768 devices in a mesh: inter: 32 (over x, z_hi, core), intra: 24 (over z_lo, y).
Axes of the slice: x: 4, y: 8, z: 12 (z_hi: 4, z_lo: 3; z = z_hi * 3 + z_lo), core: 2. Of those that a mesh axis runs over, the one named last changes fastest.
Arguments:
- tokens: bfloat16 [4608, 8192], P('intra'), may hold values from -6 to 6
- weight_codes: bfloat16 [14592, 8192], P(('inter', 'intra')), may hold values from -6 to 6
- exponents: int32 [14592, 64], P(('inter', 'intra')), may hold values from -8 to -6
- upstream: bfloat16 [4608, 14592], P('intra', 'inter'), may hold values from -6 to 6
Outputs:
- activation: bfloat16 [4608, 14592], P('intra', 'inter')
- grad_input: float32 [4608, 8192], P('intra', 'inter')
The draws below stay inside these ranges and needn't reach their ends.
All inputs are finite; a program needn't handle non-finite values.
Results may differ from the reference program's by a relative error of at most 0.018.
Values may be sent and summed in bfloat16 or wider, within the bound.
A program may use at most 64 MiB of HBM per device.

```python
import jax
import jax.numpy as jnp
from jax import lax

D = 8192
HIDDEN_UNITS = 14592
TOKENS = 4608
N_INTER = 32


def place_ends(entries, own_key, least, largest):
    index_at = [jax.random.randint(jax.random.fold_in(own_key, axis), (), 0, length) for axis, length in enumerate(entries.shape)]
    longest = entries.shape.index(max(entries.shape))
    next_to = index_at[:longest] + [(index_at[longest] + 1) % entries.shape[longest]] + index_at[longest + 1:]
    return entries.at[tuple(index_at)].set(least).at[tuple(next_to)].set(largest)


def block_levels(rng, shape, cuts, low, top_value):
    def one(axis_at, shards_of):
        heights = jax.random.uniform(jax.random.fold_in(jax.random.fold_in(rng, 6), axis_at), (shards_of,), jnp.float32, low / len(cuts), top_value / len(cuts))
        return jnp.repeat(jnp.exp(heights), shape[axis_at] // shards_of).reshape((-1,) + (1,) * (len(shape) - axis_at - 1))

    gain = one(*cuts[0])
    for cut in cuts[1:]:
        gain = gain * one(*cut)
    return gain


def scatter_about(key, extent, scale, bound, pieces=(), kind=jnp.bfloat16):
    loudness = block_levels(key, extent, pieces, -0.22, 0.18) if pieces else 1.0
    values = jax.random.normal(key, extent, jnp.float32) * scale * loudness
    return jnp.minimum(jnp.maximum(values, -bound), bound).astype(kind)


def setup_inputs(seed: int = 0) -> dict:
    seeds = jax.random.split(jax.random.key(seed), 5)
    return {
        "tokens": scatter_about(seeds[0], (TOKENS, D), 1.0, 6.0, ((0, 24),)),
        "weight_codes": scatter_about(seeds[1], (HIDDEN_UNITS, D), 1.0, 6.0, ((0, 768),)),
        "exponents": place_ends(jax.random.randint(seeds[2], (HIDDEN_UNITS, D // 128), -8, -5), jax.random.fold_in(seeds[2], 1), -8, (-5) - 1).astype(jnp.int32),
        "upstream": scatter_about(seeds[3], (TOKENS, HIDDEN_UNITS), 1.0, 6.0, ((0, 24), (1, 32))),
    }


def reference(tokens, weight_codes, exponents, upstream):
    row_count = weight_codes.shape[0]
    block_scale = jnp.exp2(exponents.astype(jnp.float32)).astype(jnp.bfloat16)
    weights = (weight_codes.reshape(row_count, D // 128, 128) * block_scale[:, :, None]).reshape(row_count, D)
    projected = jnp.dot(tokens, weights.T, preferred_element_type=jnp.float32)
    sig_value = jax.nn.sigmoid(projected)
    activation = (projected * sig_value).astype(jnp.bfloat16)
    slope_value = sig_value * (1.0 + projected * (1.0 - sig_value))
    grad_hidden = (upstream.astype(jnp.float32) * slope_value).astype(jnp.bfloat16)
    group_size = row_count // N_INTER

    def add_group(running, group_index):
        first_row = (group_index * group_size).astype(jnp.int32)
        grad_slice = lax.dynamic_slice_in_dim(grad_hidden, first_row, group_size, 1)
        weight_slice = lax.dynamic_slice_in_dim(weights, first_row, group_size, 0)
        group_term = jnp.dot(grad_slice, weight_slice, preferred_element_type=jnp.float32)
        rounded = lax.optimization_barrier(group_term.astype(jnp.bfloat16))
        return running + rounded.astype(jnp.float32), None

    initial = jnp.zeros((tokens.shape[0], D), jnp.float32)
    grad_input, _ = lax.scan(add_group, initial, jnp.arange(N_INTER, dtype=jnp.int32))
    return activation, grad_input
```

```python
import jax
import jax.numpy as jnp
from jax import lax
from jax.experimental import pallas as pl
from jax.experimental.pallas import tpu as pltpu
from jax.sharding import PartitionSpec as P

MESH = pl.DeviceIdType.MESH
F32 = jnp.float32
BF16 = jnp.bfloat16

WINDOW = 768
WIDTH = 4 * WINDOW
ROWS = 192
SLOT = 64
NT = (((1,), (1,)), ((), ()))


def slot_of(offset):
    if offset == 0:
        return 0
    return 2 * offset - 1 if offset > 0 else -2 * offset


def device(x, y, z, core):
    x, y, z, core = lax.rem(x + 8, 4), lax.rem(y + 8, 8), lax.rem(z + 24, 12), lax.rem(core + 2, 2)
    return {"inter": x * 8 + (z // 3) * 2 + core, "intra": lax.rem(z, 3) * 8 + y}


def kernel(
    tokens, codes, exponents, upstream, act_out, grad_out,
    windows, remnants, gathered, tok, perm, up_perm, p_send, p_own, p_recv, act_perm, hidden,
    g_send, g_recv, g_own, x_send, x_mid, x_recv, z_send, z_recv,
    tok_own_sem, a2a_s, a2a_r, ring_s, ring_r, tok_s, tok_r, tokc_s, tokc_r,
    p_s, p_r, h_s, h_r, g_s, g_r, m_s, m_r, x_s, x_r, f_s, f_r,
):
    inter = lax.axis_index("inter")
    intra = lax.axis_index("intra")
    x, z_hi, core = inter // 8, lax.rem(inter // 2, 4), lax.rem(inter, 2)
    j, y = intra // 8, lax.rem(intra, 8)
    z = z_hi * 3 + j
    other_core = device(x, y, z, core + 1)

    def part(m):
        return lax.rem(j + m, 3)

    def group_peer(m):
        return {"inter": inter, "intra": part(m) * 8 + y}

    def rows_of(s, size=ROWS, start=0):
        return pl.ds(pl.multiple_of(s * ROWS + start, 16), size)

    def remote(src, dst, send_sem, recv_sem, to):
        return pltpu.make_async_remote_copy(
            src_ref=src, dst_ref=dst, send_sem=send_sem, recv_sem=recv_sem,
            device_id=to, device_id_type=MESH,
        )

    pending = []

    barrier = pltpu.get_barrier_semaphore()
    peers = [device(x, y, z + dz, core + dc) for dz in range(12) for dc in range(2) if dz or dc]
    peers += [device(x, y + 1, z, core), device(x, y + 7, z, core)]
    peers += [device(x + 1, y, z, core), device(x + 3, y, z, core)]
    for peer in peers:
        pl.semaphore_signal(barrier, inc=1, device_id=peer, device_id_type=MESH)

    def token_columns(q, to_part):
        return pl.ds(pl.multiple_of(q * 2048 + to_part * 640, 128), WINDOW)

    own_copies = [
        pltpu.make_async_copy(
            tokens.at[:, token_columns(q, j)],
            tok.at[rows_of(j), pl.ds(q * WINDOW, WINDOW)],
            tok_own_sem.at[q],
        )
        for q in range(4)
    ]
    for copy in own_copies:
        copy.start()

    scale = jnp.exp2(exponents[...].astype(F32)).astype(BF16).astype(F32)
    row = lax.broadcasted_iota(jnp.int32, (16, 128), 0)
    blank = jnp.zeros((32, 128), BF16)
    for q in range(4):
        for i in range(16):
            b = q * 16 + i
            value = codes[:, b * 128:(b + 1) * 128].astype(F32) * scale[:, b:b + 1]
            tail = jnp.zeros((16, 128), F32)
            for k in range(3):
                tail = jnp.where(row == 3 * j + k, value[16 + k:17 + k, :], tail)
            to = min(i // 5, 2)
            at = q * WINDOW + (i - 5 * to) * 128
            windows[to, 0:16, at:at + 128] = value[0:16].astype(BF16)
            windows[to, 16:32, at:at + 128] = tail.astype(BF16)
        for to in range(2):
            windows[to, :, q * WINDOW + 640:(q + 1) * WINDOW] = blank
    mine = pl.ds(pl.multiple_of(16 * j, 16), 16)
    gathered[mine, :] = windows[j, 0:16, :]

    pl.semaphore_wait(barrier, len(peers))

    a2a_main, a2a_tail = [], []
    for m in (1, 2):
        a2a_main.append(remote(
            windows.at[part(m), pl.ds(0, 16)], gathered.at[mine],
            a2a_s.at[0, m - 1], a2a_r.at[0, m - 1], group_peer(m)))
        a2a_tail.append(remote(
            windows.at[part(m), pl.ds(16, 16)], remnants.at[m - 1],
            a2a_s.at[1, m - 1], a2a_r.at[1, m - 1], group_peer(m)))
    for copy in a2a_main:
        copy.start()

    def unit_rows(u, offset):
        if u == 3:
            return pl.ds(slot_of(offset) * SLOT + 48, 16)
        return pl.ds(pl.multiple_of(slot_of(offset) * SLOT + 16 * part(u), 16), 16)

    def ring(u, way, k):
        sign = 1 if way == 0 else -1
        to = 4 if k == 4 else sign * k
        return remote(
            gathered.at[unit_rows(u, sign * (k - 1))], gathered.at[unit_rows(u, to)],
            ring_s.at[u, way, k - 1], ring_r.at[u, way, k - 1], device(x, y + sign, z, core))

    def goes(u, way, k):
        return k <= 3 or (k == 4 and u % 2 == way)

    def ring_start(u, way, k):
        if goes(u, way, k):
            copy = ring(u, way, k)
            copy.start()
            pending.append(copy)

    def ring_arrive(u, k):
        for way in (0, 1):
            if goes(u, way, k):
                ring(u, way, k).wait_recv()
                ring_start(u, way, k + 1)

    def ring_open(u):
        ring_start(u, 0, 1)
        ring_start(u, 1, 1)

    ring_open(0)
    for copy in a2a_tail:
        copy.start()
    pending += a2a_main + a2a_tail

    at = lax.broadcasted_iota(jnp.int32, (512, 456), 0)
    natural = lax.broadcasted_iota(jnp.int32, (512, 456), 1)
    slot, within = at >> 6, at & 63
    offset = jnp.where((slot & 1) == 1, (slot + 1) >> 1, -(slot >> 1))
    source_y = (y - offset + 8) & 7
    late = within - 48
    late_z = (late >= 3).astype(jnp.int32) + (late >= 6).astype(jnp.int32)
    source_z = jnp.where(late < 0, within >> 4, late_z)
    source_row = jnp.where(late < 0, within & 15, 16 + late - 3 * late_z)
    matches = (natural == (source_z * 8 + source_y) * 19 + source_row) & (late < 9)
    perm[...] = jnp.where(matches, 1.0, 0.0).astype(BF16)
    up_perm[...] = lax.dot_general(upstream[...], perm[...], NT, preferred_element_type=F32)

    token_copies = []
    for way, step, to_part in ((0, 1, part(1)), (1, 11, part(2))):
        for q in range(4):
            token_copies.append(remote(
                tokens.at[pl.ds(pl.multiple_of(96 * core, 16), 96), token_columns(q, to_part)],
                tok.at[rows_of(j, 96, 96 * core), pl.ds(q * WINDOW, WINDOW)],
                tok_s.at[way, q], tok_r.at[way, q], device(x, y, z + step, core)))

    ring_arrive(0, 1)
    for u in (1, 2):
        a2a_main[2 - u].wait_recv()
        ring_open(u)
    for copy in token_copies:
        copy.start()
    pending += token_copies
    ring_arrive(0, 2)
    for copy in a2a_tail:
        copy.wait_recv()
    gathered[48:64, :] = (
        windows[j, 16:32, :].astype(F32) + remnants[0].astype(F32) + remnants[1].astype(F32)
    ).astype(BF16)
    ring_open(3)
    ring_arrive(1, 1)
    ring_arrive(2, 1)
    ring_arrive(0, 3)
    ring_arrive(3, 1)
    ring_arrive(1, 2)
    ring_arrive(2, 2)
    ring_arrive(0, 4)
    ring_arrive(3, 2)

    core_copies = []
    for way in (0, 1):
        for q in range(4):
            token_copies[way * 4 + q].wait_recv()
        block = tok.at[rows_of(part(2 - way), 96, 96 * core)]
        copy = remote(block, block, tokc_s.at[way], tokc_r.at[way], other_core)
        copy.start()
        core_copies.append(copy)
    pending += core_copies

    ring_arrive(1, 3)
    ring_arrive(2, 3)
    ring_arrive(3, 3)
    for copy in core_copies:
        copy.wait_recv()
    for copy in own_copies:
        copy.wait()

    p_copies, h_copies = {}, {}

    def project(c):
        columns = pl.ds(c * 128, 128)
        for s in range(3):
            value = lax.dot_general(
                tok[s * ROWS:(s + 1) * ROWS, :], gathered[c * 128:(c + 1) * 128, :], NT,
                preferred_element_type=F32)
            p_send[s * ROWS:(s + 1) * ROWS, columns] = value.astype(BF16)

            @pl.when(j == s)
            def _():
                p_own[:, columns] = value

        for m in (1, 2):
            copy = remote(
                p_send.at[rows_of(part(m)), columns], p_recv.at[m - 1, :, columns],
                p_s.at[c, m - 1], p_r.at[c, m - 1], group_peer(m))
            copy.start()
            p_copies[c, m] = copy
            pending.append(copy)

    def activate(c):
        columns = pl.ds(c * 128, 128)
        for m in (1, 2):
            p_copies[c, m].wait_recv()
        projected = p_own[:, columns] + p_recv[0, :, columns].astype(F32) + p_recv[1, :, columns].astype(F32)
        sig = 1.0 / (1.0 + jnp.exp(-projected))
        act_perm[:, columns] = (projected * sig).astype(BF16)
        slope = sig * (1.0 + projected * (1.0 - sig))
        hidden[rows_of(j), columns] = (up_perm[:, columns] * slope).astype(BF16)
        for m in (1, 2):
            block = hidden.at[rows_of(j), columns]
            copy = remote(block, block, h_s.at[c, m - 1], h_r.at[c, m - 1], group_peer(m))
            copy.start()
            h_copies[c, m] = copy
            pending.append(copy)

    project(0)
    project(1)
    project(2)
    activate(0)
    activate(1)
    ring_arrive(1, 4)
    ring_arrive(2, 4)
    ring_arrive(3, 4)
    project(3)
    activate(2)
    activate(3)
    act_out[...] = jnp.dot(act_perm[...], perm[...], preferred_element_type=F32).astype(BF16)
    for c in range(4):
        for m in (1, 2):
            h_copies[c, m].wait_recv()

    g_copies = []

    def half(s, q, which):
        columns = pl.ds(pl.multiple_of(q * WINDOW + 384 * which, 128), 384)
        return jnp.dot(
            hidden[s * ROWS:(s + 1) * ROWS, :], gathered[:, columns], preferred_element_type=F32)

    for s in range(3):
        for q in range(4):
            g_send[s, q] = half(s, q, 1 - core).astype(BF16)
        copy = remote(g_send.at[s], g_recv.at[s], g_s.at[s], g_r.at[s], other_core)
        copy.start()
        g_copies.append(copy)
    pending += g_copies

    right, left = device(x + 1, y, z, core), device(x + 3, y, z, core)
    far, near, back = lax.rem(x + 2, 4), lax.rem(x + 1, 4), lax.rem(x + 3, 4)
    mid_copies, x_copies = {}, {}
    for s in range(3):
        for q in range(4):
            g_own[s, q] = half(s, q, core)
        g_copies[s].wait_recv()
        for q in range(4):
            g_own[s, q] = g_own[s, q] + g_recv[s, q].astype(F32)
        x_send[s, 0] = g_own[s, far].astype(BF16)
        for way, to in ((0, right), (1, left)):
            copy = remote(
                x_send.at[s, 0, pl.ds(96 * way, 96)], x_mid.at[s, way],
                m_s.at[s, way], m_r.at[s, way], to)
            copy.start()
            mid_copies[s, way] = copy
            pending.append(copy)
    for s in range(3):
        for way, to, quarter in ((0, right, near), (1, left, back)):
            mid_copies[s, way].wait_recv()
            own, there = pl.ds(96 * way, 96), pl.ds(96 - 96 * way, 96)
            x_send[s, 1 + way, own, :] = (g_own[s, quarter, own, :] + x_mid[s, way].astype(F32)).astype(BF16)
            x_send[s, 1 + way, there, :] = g_own[s, quarter, there, :].astype(BF16)
            copy = remote(x_send.at[s, 1 + way], x_recv.at[s, way], x_s.at[s, way], x_r.at[s, way], to)
            copy.start()
            x_copies[s, way] = copy
            pending.append(copy)

    last = []
    for s in range(3):
        for way in (0, 1):
            x_copies[s, way].wait_recv()
        z_send[s] = (g_own[s, x] + x_recv[s, 0].astype(F32) + x_recv[s, 1].astype(F32)).astype(BF16)
        for i in range(3):
            block = 5 * j + 3 * core + i
            owner, side = block // 2, lax.rem(block, 2)
            valid = jnp.logical_or(core == 0, j == 2) if i == 2 else True
            here = jnp.logical_and(owner == z_hi * 2 + core, j == s)
            src = z_send.at[s, :, pl.ds(128 * i, 128)]
            dst = z_recv.at[z_hi, :, pl.ds(pl.multiple_of(128 * side, 128), 128)]
            away = remote(
                src, dst, f_s.at[s, i], f_r.at[z_hi, side],
                {"inter": x * 8 + owner, "intra": s * 8 + y})
            stay = pltpu.make_async_copy(src, dst, f_r.at[z_hi, side])
            leaves = jnp.logical_and(valid, jnp.logical_not(here))

            @pl.when(leaves)
            def _():
                away.start()

            @pl.when(jnp.logical_and(valid, here))
            def _():
                stay.start()

            last.append((leaves, away))

    for copy in pending:
        copy.wait_send()
    for leaves, copy in last:
        @pl.when(leaves)
        def _():
            copy.wait_send()

    for source in range(4):
        for side in range(2):
            piece = z_recv.at[source, :, pl.ds(128 * side, 128)]
            pltpu.make_async_copy(piece, piece, f_r.at[source, side]).wait()
    grad_out[...] = (
        (z_recv[0].astype(F32) + z_recv[1].astype(F32)) + (z_recv[2].astype(F32) + z_recv[3].astype(F32))
    )


def per_device(tokens, weight_codes, exponents, upstream):
    vmem = pl.BlockSpec(memory_space=pltpu.VMEM)
    dma = pltpu.SemaphoreType.DMA
    return pl.pallas_call(
        kernel,
        out_shape=(
            jax.ShapeDtypeStruct((ROWS, 456), BF16),
            jax.ShapeDtypeStruct((ROWS, 256), F32),
        ),
        in_specs=[pl.BlockSpec(memory_space=pl.ANY), vmem, vmem, vmem],
        out_specs=(vmem, vmem),
        scratch_shapes=[
            pltpu.VMEM((3, 32, WIDTH), BF16),
            pltpu.VMEM((2, 16, WIDTH), BF16),
            pltpu.VMEM((512, WIDTH), BF16),
            pltpu.VMEM((3 * ROWS, WIDTH), BF16),
            pltpu.VMEM((512, 456), BF16),
            pltpu.VMEM((ROWS, 512), F32),
            pltpu.VMEM((3 * ROWS, 512), BF16),
            pltpu.VMEM((ROWS, 512), F32),
            pltpu.VMEM((2, ROWS, 512), BF16),
            pltpu.VMEM((ROWS, 512), BF16),
            pltpu.VMEM((3 * ROWS, 512), BF16),
            pltpu.VMEM((3, 4, ROWS, 384), BF16),
            pltpu.VMEM((3, 4, ROWS, 384), BF16),
            pltpu.VMEM((3, 4, ROWS, 384), F32),
            pltpu.VMEM((3, 3, ROWS, 384), BF16),
            pltpu.VMEM((3, 2, 96, 384), BF16),
            pltpu.VMEM((3, 2, ROWS, 384), BF16),
            pltpu.VMEM((3, ROWS, 384), BF16),
            pltpu.VMEM((4, ROWS, 256), BF16),
            dma((4,)),
            dma((2, 2)), dma((2, 2)),
            dma((4, 2, 4)), dma((4, 2, 4)),
            dma((2, 4)), dma((2, 4)),
            dma((2,)), dma((2,)),
            dma((4, 2)), dma((4, 2)),
            dma((4, 2)), dma((4, 2)),
            dma((3,)), dma((3,)),
            dma((3, 2)), dma((3, 2)),
            dma((3, 2)), dma((3, 2)),
            dma((3, 3)), dma((4, 2)),
        ],
        compiler_params=pltpu.CompilerParams(
            collective_id=0, has_side_effects=True, vmem_limit_bytes=48 << 20),
        cost_estimate=pl.CostEstimate(
            flops=4 * ROWS * 8192 * 456, bytes_accessed=8 << 20, transcendentals=ROWS * 512),
    )(tokens, weight_codes, exponents, upstream)


def solution(mesh):
    placed = (
        P("intra", None),
        P(("inter", "intra"), None),
        P(("inter", "intra"), None),
        P("intra", "inter"),
    )
    return jax.shard_map(
        per_device,
        mesh=mesh,
        in_specs=placed,
        out_specs=(P("intra", "inter"), P("intra", "inter")),
        check_vma=False,
    )
```

```python
import jax
import jax.numpy as jnp
from jax import lax
from jax.experimental import pallas as pl
from jax.experimental.pallas import tpu as pltpu
from jax.sharding import PartitionSpec as P

MESH = pl.DeviceIdType.MESH
F32 = jnp.float32
BF16 = jnp.bfloat16

WINDOW = 768
WIDTH = 4 * WINDOW
ROWS = 192
SLOT = 64
PACK = 640
UNIT = WIDTH + PACK
PIECE = 96
CHUNKS = ((0, 256), (256, 128), (384, 128))
NT = (((1,), (1,)), ((), ()))


def slot_of(offset):
    if offset == 0:
        return 0
    return 2 * offset - 1 if offset > 0 else -2 * offset


def device(x, y, z, core):
    x, y, z, core = lax.rem(x + 8, 4), lax.rem(y + 8, 8), lax.rem(z + 24, 12), lax.rem(core + 2, 2)
    return {"inter": x * 8 + (z // 3) * 2 + core, "intra": lax.rem(z, 3) * 8 + y}


def kernel(
    tokens, codes_hbm, exponents_hbm, upstream_hbm, act_out, grad_out,
    codes, exponents, upstream,
    windows, packed, gathered, tok, perm, up_perm, p_part, p_send, p_recv, act_perm, hidden,
    g_send, g_recv, g_own, x_far, x_send, x_mid, x_recv, z_send, z_recv,
    load_sem, tok_own_sem, a2a_s, a2a_r, ring_s, ring_r, tok_s, tok_r, tokc_s, tokc_r,
    p_s, p_r, h_s, h_r, g_s, g_r, m_s, m_r, n_s, n_r, x_s, x_r, f_s, f_r,
):
    inter = lax.axis_index("inter")
    intra = lax.axis_index("intra")
    x, z_hi, core = inter // 8, lax.rem(inter // 2, 4), lax.rem(inter, 2)
    j, y = intra // 8, lax.rem(intra, 8)
    z = z_hi * 3 + j
    other_core = device(x, y, z, core + 1)

    def part(m):
        return lax.rem(j + m, 3)

    def group_peer(m):
        return {"inter": inter, "intra": part(m) * 8 + y}

    def rows_of(s, size=ROWS, start=0):
        return pl.ds(pl.multiple_of(s * ROWS + start, 16), size)

    def remote(src, dst, send_sem, recv_sem, to):
        return pltpu.make_async_remote_copy(
            src_ref=src, dst_ref=dst, send_sem=send_sem, recv_sem=recv_sem,
            device_id=to, device_id_type=MESH,
        )

    pending = []

    def launch(copy):
        copy.start()
        pending.append(copy)
        return copy

    barrier = pltpu.get_barrier_semaphore()
    peers = [device(x, y, z + dz, core + dc) for dz in range(12) for dc in range(2) if dz or dc]
    peers += [device(x, y + 1, z, core), device(x, y + 7, z, core)]
    peers += [device(x + 1, y, z, core), device(x + 3, y, z, core)]
    for peer in peers:
        pl.semaphore_signal(barrier, inc=1, device_id=peer, device_id_type=MESH)

    loads = [
        pltpu.make_async_copy(src, dst, load_sem.at[i])
        for i, (src, dst) in enumerate(
            ((codes_hbm, codes), (exponents_hbm, exponents), (upstream_hbm, upstream)))
    ]
    for copy in loads:
        copy.start()

    def token_columns(q, to_part):
        return pl.ds(pl.multiple_of(q * 2048 + to_part * 640, 128), WINDOW)

    own_copies = [
        pltpu.make_async_copy(
            tokens.at[:, token_columns(q, j)],
            tok.at[rows_of(j), pl.ds(q * WINDOW, WINDOW)],
            tok_own_sem.at[q],
        )
        for q in range(4)
    ]
    for copy in own_copies:
        copy.start()

    packed[...] = jnp.zeros_like(packed)
    loads[0].wait()
    loads[1].wait()
    scale = jnp.exp2(exponents[...].astype(F32)).astype(BF16).astype(F32)
    blank = jnp.zeros((16, 128), BF16)
    for q in range(4):
        for i in range(16):
            b = q * 16 + i
            value = codes[:, b * 128:(b + 1) * 128].astype(F32) * scale[:, b:b + 1]
            to = min(i // 5, 2)
            at = q * 6 + i - 5 * to
            windows[to, :, at * 128:(at + 1) * 128] = value[0:16].astype(BF16)
            run, lane = 3 * (at // 5), at % 5 * 128
            packed[to, run:run + 3, lane:lane + 128] = value[16:19]
        for to in range(2):
            windows[to, :, q * WINDOW + 640:(q + 1) * WINDOW] = blank
    for to in range(3):
        windows[to, :, WIDTH:] = packed[to].astype(BF16)
    mine = pl.ds(pl.multiple_of(16 * j, 16), 16)
    gathered[mine, :] = windows[j]

    pl.semaphore_wait(barrier, len(peers))

    a2a = [
        launch(remote(
            windows.at[part(m)], gathered.at[mine], a2a_s.at[m - 1], a2a_r.at[m - 1], group_peer(m)))
        for m in (1, 2)
    ]

    def unit_rows(u, slot):
        return pl.ds(pl.multiple_of(slot * SLOT + 16 * part(u), 16), 16)

    def ring(u, way, k):
        sign = 1 if way == 0 else -1
        return remote(
            gathered.at[unit_rows(u, slot_of(sign * (k - 1)))],
            gathered.at[unit_rows(u, slot_of(sign * k))],
            ring_s.at[u, way, k - 1], ring_r.at[u, way, k - 1], device(x, y + sign, z, core))

    def ring_last(u):
        odd = lax.rem(core + u, 2)
        return remote(
            gathered.at[unit_rows(u, slot_of(3) + odd)], gathered.at[unit_rows(u, slot_of(4))],
            ring_s.at[u, 0, 3], ring_r.at[u, 0, 3], device(x, y + 1 - 2 * odd, z, core))

    def ring_open(u):
        for way in (0, 1):
            launch(ring(u, way, 1))

    def ring_arrive(u, k):
        if k == 4:
            ring_last(u).wait_recv()
            return
        for way in (0, 1):
            ring(u, way, k).wait_recv()
            if k < 3:
                launch(ring(u, way, k + 1))
        if k == 3:
            launch(ring_last(u))

    ring_open(0)

    at = lax.broadcasted_iota(jnp.int32, (512, 456), 0)
    natural = lax.broadcasted_iota(jnp.int32, (512, 456), 1)
    slot, within = at >> 6, at & 63
    offset = jnp.where((slot & 1) == 1, (slot + 1) >> 1, -(slot >> 1))
    source_y = (y - offset + 8) & 7
    late = within - 48
    late_z = (late >= 3).astype(jnp.int32) + (late >= 6).astype(jnp.int32)
    source_z = jnp.where(late < 0, within >> 4, late_z)
    source_row = jnp.where(late < 0, within & 15, 16 + late - 3 * late_z)
    matches = (natural == (source_z * 8 + source_y) * 19 + source_row) & (late < 9)
    perm[...] = jnp.where(matches, 1.0, 0.0).astype(BF16)
    loads[2].wait()
    up_perm[...] = lax.dot_general(upstream[...], perm[...], NT, preferred_element_type=F32)

    to_row = lax.broadcasted_iota(jnp.int32, (80, 48), 0)
    from_row = lax.broadcasted_iota(jnp.int32, (80, 48), 1)
    run, within = to_row >> 4, to_row & 15
    late_z = (within >= 3).astype(jnp.int32) + (within >= 6).astype(jnp.int32)
    matches = (from_row == 16 * late_z + 3 * run + within - 3 * late_z) & (within < 9)
    unpacker = jnp.where(matches, 1.0, 0.0).astype(BF16)

    def unpack(offset):
        top = slot_of(offset) * SLOT
        rows = jnp.dot(unpacker, gathered[top:top + 48, WIDTH:], preferred_element_type=F32).astype(BF16)
        for c in range(5):
            width = min(PACK, WIDTH - c * PACK)
            gathered[top + 48:top + 64, c * PACK:c * PACK + width] = rows[16 * c:16 * c + 16, :width]

    token_copies = []
    for way, step, to_part in ((0, 1, part(1)), (1, 11, part(2))):
        for q in range(4):
            token_copies.append(remote(
                tokens.at[pl.ds(pl.multiple_of(96 * core, 16), 96), token_columns(q, to_part)],
                tok.at[rows_of(j, 96, 96 * core), pl.ds(q * WINDOW, WINDOW)],
                tok_s.at[way, q], tok_r.at[way, q], device(x, y, z + step, core)))

    def project(c, rows):
        start, width = CHUNKS[c]
        p_part[rows, pl.ds(start, width)] = lax.dot_general(
            tok[rows, :], gathered[start:start + width, :WIDTH], NT, preferred_element_type=F32)

    def offer(c):
        columns = pl.ds(*CHUNKS[c])
        for m in (1, 2):
            p_send[m - 1, :, columns] = p_part[rows_of(part(m)), columns].astype(BF16)
            p_copies[c, m] = launch(remote(
                p_send.at[m - 1, :, columns], p_recv.at[m - 1, :, columns],
                p_s.at[c, m - 1], p_r.at[c, m - 1], group_peer(m)))

    def activate(c):
        columns = pl.ds(*CHUNKS[c])
        for m in (1, 2):
            p_copies[c, m].wait_recv()
        projected = p_part[rows_of(j), columns] + p_recv[0, :, columns].astype(F32) + p_recv[1, :, columns].astype(F32)
        sig = 1.0 / (1.0 + jnp.exp(-projected))
        slope = sig * (1.0 + projected * (1.0 - sig))
        hidden[rows_of(j), columns] = (up_perm[:, columns] * slope).astype(BF16)
        block = hidden.at[rows_of(j), columns]
        for m in (1, 2):
            h_copies.append(launch(remote(
                block, block, h_s.at[c, m - 1], h_r.at[c, m - 1], group_peer(m))))
        act_perm[:, columns] = (projected * sig).astype(BF16)

    p_copies, h_copies = {}, []

    ring_arrive(0, 1)
    for u in (1, 2):
        a2a[2 - u].wait_recv()
        ring_open(u)
    for copy in token_copies:
        launch(copy)
    unpack(0)
    ring_arrive(0, 2)
    ring_arrive(1, 1)
    ring_arrive(2, 1)
    unpack(1)
    unpack(-1)
    ring_arrive(0, 3)
    ring_arrive(1, 2)
    ring_arrive(2, 2)
    unpack(2)
    unpack(-2)
    for copy in own_copies:
        copy.wait()
    project(0, rows_of(j))

    core_copies = []
    for way in (0, 1):
        for q in range(4):
            token_copies[way * 4 + q].wait_recv()
        block = tok.at[rows_of(part(2 - way), 96, 96 * core)]
        core_copies.append(launch(remote(block, block, tokc_s.at[way], tokc_r.at[way], other_core)))

    ring_arrive(0, 4)
    ring_arrive(1, 3)
    for copy in core_copies:
        copy.wait_recv()
    project(0, rows_of(part(1)))
    project(0, rows_of(part(2)))
    offer(0)
    ring_arrive(2, 3)
    unpack(3)
    unpack(-3)
    project(1, slice(None))
    offer(1)
    activate(0)
    ring_arrive(1, 4)
    ring_arrive(2, 4)
    unpack(4)
    project(2, slice(None))
    offer(2)
    activate(1)
    activate(2)
    act_out[...] = jnp.dot(act_perm[...], perm[...], preferred_element_type=F32).astype(BF16)
    for copy in h_copies:
        copy.wait_recv()

    quarters = [lax.rem(x + 2, 4), lax.rem(x + 1, 4), lax.rem(x + 3, 4), x]
    g_copies = []

    def half(i, rows, which):
        columns = pl.ds(pl.multiple_of(quarters[i] * WINDOW + 384 * which, 128), 384)
        return jnp.dot(hidden[rows, :], gathered[:, columns], preferred_element_type=F32)

    def give(i, rows):
        g_send[i, rows, :] = half(i, rows, 1 - core).astype(BF16)
        n = len(g_copies)
        g_copies.append(launch(remote(
            g_send.at[i, rows], g_recv.at[i, rows], g_s.at[n], g_r.at[n], other_core)))

    def keep(i):
        g_own[i] = half(i, pl.ds(0, 3 * ROWS), core)

    def pair_sum(i, rows):
        return g_own[i, rows, :] + g_recv[i, rows, :].astype(F32)

    pieces = 3 * ROWS // PIECE
    sides = (x + 1, x + 3)
    far_copies, near_copies, mid_copies = {}, {}, {}

    def rows_at(p, part_of=None):
        if part_of is None:
            return pl.ds(p * PIECE, PIECE)
        return pl.ds(p * PIECE + part_of * (PIECE // 2), PIECE // 2)

    def send_far(p):
        x_far[rows_at(p), :] = pair_sum(0, rows_at(p)).astype(BF16)
        for way in (0, 1):
            far_copies[p, way] = launch(remote(
                x_far.at[rows_at(p, way)], x_mid.at[rows_at(p, way)],
                m_s.at[p, way], m_r.at[p, way], device(sides[way], y, z, core)))

    def send_near(p):
        for way in (0, 1):
            rows = rows_at(p, 1 - way)
            x_send[way, rows, :] = pair_sum(1 + way, rows).astype(BF16)
            near_copies[p, way] = launch(remote(
                x_send.at[way, rows], x_recv.at[way, rows],
                n_s.at[p, way], n_r.at[p, way], device(sides[way], y, z, core)))

    def send_mid(p):
        for way in (0, 1):
            rows = rows_at(p, way)
            far_copies[p, way].wait_recv()
            x_send[way, rows, :] = (pair_sum(1 + way, rows) + x_mid[rows, :].astype(F32)).astype(BF16)
            mid_copies[p, way] = launch(remote(
                x_send.at[way, rows], x_recv.at[way, rows],
                x_s.at[p, way], x_r.at[p, way], device(sides[way], y, z, core)))

    leaving = []

    def send_owner(p):
        for way in (0, 1):
            near_copies[p, way].wait_recv()
            mid_copies[p, way].wait_recv()
        rows = rows_at(p)
        z_send[rows, :] = (
            pair_sum(3, rows) + x_recv[0, rows, :].astype(F32) + x_recv[1, rows, :].astype(F32)
        ).astype(BF16)
        s, there = p * PIECE // ROWS, p * PIECE % ROWS
        for i in range(3):
            block = 5 * j + 3 * core + i
            owner, side = block // 2, lax.rem(block, 2)
            valid = jnp.logical_or(core == 0, j == 2) if i == 2 else True
            here = jnp.logical_and(owner == z_hi * 2 + core, j == s)
            src = z_send.at[rows, pl.ds(128 * i, 128)]
            dst = z_recv.at[z_hi, pl.ds(there, PIECE), pl.ds(pl.multiple_of(128 * side, 128), 128)]
            arrived = f_r.at[z_hi, side, there // PIECE]
            away = remote(
                src, dst, f_s.at[p, i], arrived, {"inter": x * 8 + owner, "intra": s * 8 + y})
            stay = pltpu.make_async_copy(src, dst, arrived)
            leaves = jnp.logical_and(valid, jnp.logical_not(here))

            @pl.when(leaves)
            def _():
                away.start()

            @pl.when(jnp.logical_and(valid, here))
            def _():
                stay.start()

            leaving.append((leaves, away))

    every = pl.ds(0, 3 * ROWS)
    give(0, pl.ds(0, 288))
    give(0, pl.ds(288, 288))
    keep(0)
    give(1, every)
    give(2, every)
    g_copies[0].wait_recv()
    send_far(0)
    send_far(1)
    keep(1)
    keep(2)
    g_copies[1].wait_recv()
    g_copies[2].wait_recv()
    g_copies[3].wait_recv()
    send_near(0)
    send_near(1)
    give(3, every)
    send_mid(0)
    send_mid(1)
    send_far(2)
    send_far(3)
    send_near(2)
    keep(3)
    g_copies[4].wait_recv()
    send_owner(0)
    send_near(3)
    send_mid(2)
    send_owner(1)
    send_mid(3)
    send_far(4)
    send_far(5)
    send_near(4)
    send_owner(2)
    send_near(5)
    send_mid(4)
    send_owner(3)
    send_mid(5)
    send_owner(4)
    send_owner(5)

    for copy in pending:
        copy.wait_send()
    for leaves, copy in leaving:
        @pl.when(leaves)
        def _():
            copy.wait_send()

    total = None
    for source in range(4):
        for side in range(2):
            for part_of in range(ROWS // PIECE):
                piece = z_recv.at[source, pl.ds(PIECE * part_of, PIECE), pl.ds(128 * side, 128)]
                pltpu.make_async_copy(piece, piece, f_r.at[source, side, part_of]).wait()
        value = z_recv[source].astype(F32)
        total = value if total is None else total + value
    grad_out[...] = total


def per_device(tokens, weight_codes, exponents, upstream):
    vmem = pl.BlockSpec(memory_space=pltpu.VMEM)
    hbm = pl.BlockSpec(memory_space=pltpu.HBM)
    dma = pltpu.SemaphoreType.DMA
    pieces = 3 * ROWS // PIECE
    return pl.pallas_call(
        kernel,
        out_shape=(
            jax.ShapeDtypeStruct((ROWS, 456), BF16),
            jax.ShapeDtypeStruct((ROWS, 256), F32),
        ),
        in_specs=[hbm] * 4,
        out_specs=(vmem, vmem),
        scratch_shapes=[
            pltpu.VMEM((19, 8192), BF16),
            pltpu.VMEM((19, 64), jnp.int32),
            pltpu.VMEM((ROWS, 456), BF16),
            pltpu.VMEM((3, 16, UNIT), BF16),
            pltpu.VMEM((3, 16, PACK), F32),
            pltpu.VMEM((512, UNIT), BF16),
            pltpu.VMEM((3 * ROWS, WIDTH), BF16),
            pltpu.VMEM((512, 456), BF16),
            pltpu.VMEM((ROWS, 512), F32),
            pltpu.VMEM((3 * ROWS, 512), F32),
            pltpu.VMEM((2, ROWS, 512), BF16),
            pltpu.VMEM((2, ROWS, 512), BF16),
            pltpu.VMEM((ROWS, 512), BF16),
            pltpu.VMEM((3 * ROWS, 512), BF16),
            pltpu.VMEM((4, 3 * ROWS, 384), BF16),
            pltpu.VMEM((4, 3 * ROWS, 384), BF16),
            pltpu.VMEM((4, 3 * ROWS, 384), F32),
            pltpu.VMEM((3 * ROWS, 384), BF16),
            pltpu.VMEM((2, 3 * ROWS, 384), BF16),
            pltpu.VMEM((3 * ROWS, 384), BF16),
            pltpu.VMEM((2, 3 * ROWS, 384), BF16),
            pltpu.VMEM((3 * ROWS, 384), BF16),
            pltpu.VMEM((4, ROWS, 256), BF16),
            dma((3,)), dma((4,)),
            dma((2,)), dma((2,)),
            dma((3, 2, 4)), dma((3, 2, 4)),
            dma((2, 4)), dma((2, 4)),
            dma((2,)), dma((2,)),
            dma((3, 2)), dma((3, 2)),
            dma((3, 2)), dma((3, 2)),
            dma((5,)), dma((5,)),
            dma((pieces, 2)), dma((pieces, 2)),
            dma((pieces, 2)), dma((pieces, 2)),
            dma((pieces, 2)), dma((pieces, 2)),
            dma((pieces, 3)), dma((4, 2, ROWS // PIECE)),
        ],
        compiler_params=pltpu.CompilerParams(
            collective_id=0, has_side_effects=True, vmem_limit_bytes=48 << 20),
        cost_estimate=pl.CostEstimate(
            flops=4 * ROWS * 8192 * 456, bytes_accessed=8 << 20, transcendentals=ROWS * 512),
    )(tokens, weight_codes, exponents, upstream)


def solution(mesh):
    placed = (
        P("intra", None),
        P(("inter", "intra"), None),
        P(("inter", "intra"), None),
        P("intra", "inter"),
    )
    return jax.shard_map(
        per_device,
        mesh=mesh,
        in_specs=placed,
        out_specs=(P("intra", "inter"), P("intra", "inter")),
        check_vma=False,
    )
```

```python
import jax
import jax.numpy as jnp
from jax import lax
from jax.experimental import pallas as pl
from jax.experimental.pallas import tpu as pltpu
from jax.sharding import PartitionSpec as P

MESH = pl.DeviceIdType.MESH
F32 = jnp.float32
BF16 = jnp.bfloat16

WINDOW = 768
WIDTH = 4 * WINDOW
ROWS = 192
SLOT = 64
PACK = 640
UNIT = WIDTH + PACK
AHEAD = 2
PIECE = 96
CHUNKS = ((0, 256), (256, 128), (384, 128))
NT = (((1,), (1,)), ((), ()))


def slot_of(offset):
    if offset == 0:
        return 0
    return 2 * offset - 1 if offset > 0 else -2 * offset


def device(x, y, z, core):
    x, y, z, core = lax.rem(x + 8, 4), lax.rem(y + 8, 8), lax.rem(z + 24, 12), lax.rem(core + 2, 2)
    return {"inter": x * 8 + (z // 3) * 2 + core, "intra": lax.rem(z, 3) * 8 + y}


def kernel(
    tokens, codes_hbm, exponents_hbm, upstream_hbm, act_out, grad_out,
    codes, exponents, upstream,
    windows, packed, gathered, tok, perm, up_perm, p_part, p_send, p_recv, act_perm, hidden,
    g_send, g_recv, g_own, x_far, x_send, x_mid, x_recv, z_send, z_recv,
    load_sem, tok_own_sem, a2a_s, a2a_r, ring_s, ring_r, tok_s, tok_r, tokx_s, tokx_r, tokc_s, tokc_r,
    p_s, p_r, h_s, h_r, g_s, g_r, m_s, m_r, n_s, n_r, x_s, x_r, f_s, f_r,
):
    inter = lax.axis_index("inter")
    intra = lax.axis_index("intra")
    x, z_hi, core = inter // 8, lax.rem(inter // 2, 4), lax.rem(inter, 2)
    j, y = intra // 8, lax.rem(intra, 8)
    z = z_hi * 3 + j
    other_core = device(x, y, z, core + 1)

    def part(m):
        return lax.rem(j + m, 3)

    def group_peer(m):
        return {"inter": inter, "intra": part(m) * 8 + y}

    def rows_of(s, size=ROWS, start=0):
        return pl.ds(pl.multiple_of(s * ROWS + start, 16), size)

    def remote(src, dst, send_sem, recv_sem, to):
        return pltpu.make_async_remote_copy(
            src_ref=src, dst_ref=dst, send_sem=send_sem, recv_sem=recv_sem,
            device_id=to, device_id_type=MESH,
        )

    pending = []

    def launch(copy):
        copy.start()
        pending.append(copy)
        return copy

    barrier = pltpu.get_barrier_semaphore()
    peers = [device(x, y, z + dz, core + dc) for dz in range(12) for dc in range(2) if dz or dc]
    peers += [device(x, y + 1, z, core), device(x, y + 7, z, core)]
    peers += [device(x + 1, y, z, core), device(x + 3, y, z, core)]
    for peer in peers:
        pl.semaphore_signal(barrier, inc=1, device_id=peer, device_id_type=MESH)

    loads = [
        pltpu.make_async_copy(src, dst, load_sem.at[i])
        for i, (src, dst) in enumerate(
            ((codes_hbm, codes), (exponents_hbm, exponents), (upstream_hbm, upstream)))
    ]
    for copy in loads:
        copy.start()

    def token_columns(q, to_part):
        return pl.ds(pl.multiple_of(q * 2048 + to_part * 640, 128), WINDOW)

    own_copies = [
        pltpu.make_async_copy(
            tokens.at[:, token_columns(q, j)],
            tok.at[rows_of(j), pl.ds(q * WINDOW, WINDOW)],
            tok_own_sem.at[q],
        )
        for q in range(4)
    ]
    for copy in own_copies:
        copy.start()

    packed[...] = jnp.zeros_like(packed)
    loads[0].wait()
    loads[1].wait()
    scale = jnp.exp2(exponents[...].astype(F32)).astype(BF16).astype(F32)
    blank = jnp.zeros((16, 128), BF16)
    for q in range(4):
        for i in range(16):
            b = q * 16 + i
            value = codes[:, b * 128:(b + 1) * 128].astype(F32) * scale[:, b:b + 1]
            to = min(i // 5, 2)
            at = q * 6 + i - 5 * to
            windows[to, :, at * 128:(at + 1) * 128] = value[0:16].astype(BF16)
            run, lane = 3 * (at // 5), at % 5 * 128
            packed[to, run:run + 3, lane:lane + 128] = value[16:19]
        for to in range(2):
            windows[to, :, q * WINDOW + 640:(q + 1) * WINDOW] = blank
    for to in range(3):
        windows[to, :, WIDTH:] = packed[to].astype(BF16)
    mine = pl.ds(pl.multiple_of(16 * j, 16), 16)
    gathered[mine, :] = windows[j]

    pl.semaphore_wait(barrier, len(peers))

    a2a = [
        launch(remote(
            windows.at[part(m)], gathered.at[mine], a2a_s.at[m - 1], a2a_r.at[m - 1], group_peer(m)))
        for m in (1, 2)
    ]

    def unit_rows(u, slot):
        return pl.ds(pl.multiple_of(slot * SLOT + 16 * part(u), 16), 16)

    def ring(u, way, k):
        sign = 1 if way == 0 else -1
        return remote(
            gathered.at[unit_rows(u, slot_of(sign * (k - 1)))],
            gathered.at[unit_rows(u, slot_of(sign * k))],
            ring_s.at[u, way, k - 1], ring_r.at[u, way, k - 1], device(x, y + sign, z, core))

    def ring_last(u):
        odd = lax.rem(core + u, 2)
        return remote(
            gathered.at[unit_rows(u, slot_of(3) + odd)], gathered.at[unit_rows(u, slot_of(4))],
            ring_s.at[u, 0, 3], ring_r.at[u, 0, 3], device(x, y + 1 - 2 * odd, z, core))

    leaving_to = ([], [])

    def ring_launch(copy, ways):
        for way in ways:
            if len(leaving_to[way]) >= AHEAD:
                leaving_to[way].pop(0).wait_send()
            leaving_to[way].append(copy)
        copy.start()

    def ring_open(u):
        for way in (0, 1):
            ring_launch(ring(u, way, 1), (way,))

    def ring_arrive(u, k):
        if k == 4:
            ring_last(u).wait_recv()
            return
        for way in (0, 1):
            ring(u, way, k).wait_recv()
            if k < 3:
                ring_launch(ring(u, way, k + 1), (way,))
        if k == 3:
            launch(ring_last(u))

    ring_open(0)

    at = lax.broadcasted_iota(jnp.int32, (512, 456), 0)
    natural = lax.broadcasted_iota(jnp.int32, (512, 456), 1)
    slot, within = at >> 6, at & 63
    offset = jnp.where((slot & 1) == 1, (slot + 1) >> 1, -(slot >> 1))
    source_y = (y - offset + 8) & 7
    late = within - 48
    late_z = (late >= 3).astype(jnp.int32) + (late >= 6).astype(jnp.int32)
    source_z = jnp.where(late < 0, within >> 4, late_z)
    source_row = jnp.where(late < 0, within & 15, 16 + late - 3 * late_z)
    matches = (natural == (source_z * 8 + source_y) * 19 + source_row) & (late < 9)
    perm[...] = jnp.where(matches, 1.0, 0.0).astype(BF16)
    loads[2].wait()
    up_perm[...] = lax.dot_general(upstream[...], perm[...], NT, preferred_element_type=F32)

    to_row = lax.broadcasted_iota(jnp.int32, (80, 48), 0)
    from_row = lax.broadcasted_iota(jnp.int32, (80, 48), 1)
    run, within = to_row >> 4, to_row & 15
    late_z = (within >= 3).astype(jnp.int32) + (within >= 6).astype(jnp.int32)
    matches = (from_row == 16 * late_z + 3 * run + within - 3 * late_z) & (within < 9)
    unpacker = jnp.where(matches, 1.0, 0.0).astype(BF16)

    def unpack(offset):
        top = slot_of(offset) * SLOT
        rows = jnp.dot(unpacker, gathered[top:top + 48, WIDTH:], preferred_element_type=F32).astype(BF16)
        for c in range(5):
            width = min(PACK, WIDTH - c * PACK)
            gathered[top + 48:top + 64, c * PACK:c * PACK + width] = rows[16 * c:16 * c + 16, :width]

    quarter = 96 * core + 48 * lax.rem(x, 2)
    token_copies, side_copies, core_copies = {}, {}, {}

    def tokens_ask(q):
        for way, step, to_part in ((0, 1, part(1)), (1, 11, part(2))):
            token_copies[way, q] = launch(remote(
                tokens.at[pl.ds(pl.multiple_of(quarter, 16), 48), token_columns(q, to_part)],
                tok.at[rows_of(j, 48, quarter), pl.ds(q * WINDOW, WINDOW)],
                tok_s.at[way, q], tok_r.at[way, q], device(x, y, z + step, core)))

    def tokens_aside(q):
        for way, step in ((0, 1), (1, 3)):
            token_copies[way, q].wait_recv()
            block = tok.at[rows_of(part(2 - way), 48, quarter), pl.ds(q * WINDOW, WINDOW)]
            side_copies[way, q] = launch(remote(
                block, block, tokx_s.at[way, q], tokx_r.at[way, q], device(x + step, y, z, core)))

    def tokens_across(q):
        for way in (0, 1):
            side_copies[way, q].wait_recv()
            block = tok.at[rows_of(part(2 - way), 96, 96 * core), pl.ds(q * WINDOW, WINDOW)]
            core_copies[way, q] = launch(remote(
                block, block, tokc_s.at[way, q], tokc_r.at[way, q], other_core))

    def project(c, rows):
        start, width = CHUNKS[c]
        p_part[rows, pl.ds(start, width)] = lax.dot_general(
            tok[rows, :], gathered[start:start + width, :WIDTH], NT, preferred_element_type=F32)

    def offer(c):
        columns = pl.ds(*CHUNKS[c])
        for m in (1, 2):
            p_send[m - 1, :, columns] = p_part[rows_of(part(m)), columns].astype(BF16)
            p_copies[c, m] = launch(remote(
                p_send.at[m - 1, :, columns], p_recv.at[m - 1, :, columns],
                p_s.at[c, m - 1], p_r.at[c, m - 1], group_peer(m)))

    def activate(c):
        columns = pl.ds(*CHUNKS[c])
        for m in (1, 2):
            p_copies[c, m].wait_recv()
        projected = p_part[rows_of(j), columns] + p_recv[0, :, columns].astype(F32) + p_recv[1, :, columns].astype(F32)
        sig = 1.0 / (1.0 + jnp.exp(-projected))
        slope = sig * (1.0 + projected * (1.0 - sig))
        hidden[rows_of(j), columns] = (up_perm[:, columns] * slope).astype(BF16)
        block = hidden.at[rows_of(j), columns]
        for m in (1, 2):
            h_copies.append(launch(remote(
                block, block, h_s.at[c, m - 1], h_r.at[c, m - 1], group_peer(m))))
        act_perm[:, columns] = (projected * sig).astype(BF16)

    p_copies, h_copies = {}, []

    ring_arrive(0, 1)
    for u in (1, 2):
        a2a[2 - u].wait_recv()
        ring_open(u)
    for q in range(4):
        tokens_ask(q)
    unpack(0)
    ring_arrive(0, 2)
    tokens_aside(0)
    ring_arrive(1, 1)
    tokens_aside(1)
    ring_arrive(2, 1)
    tokens_aside(2)
    unpack(1)
    unpack(-1)
    tokens_aside(3)
    tokens_across(0)
    ring_arrive(0, 3)
    tokens_across(1)
    tokens_across(2)
    ring_arrive(1, 2)
    tokens_across(3)
    ring_arrive(2, 2)
    unpack(2)
    unpack(-2)
    for copy in own_copies:
        copy.wait()
    project(0, rows_of(j))
    ring_arrive(0, 4)
    for copy in core_copies.values():
        copy.wait_recv()
    project(0, rows_of(part(1)))
    project(0, rows_of(part(2)))
    offer(0)
    ring_arrive(1, 3)
    ring_arrive(2, 3)
    unpack(3)
    unpack(-3)
    project(1, slice(None))
    offer(1)
    activate(0)
    ring_arrive(1, 4)
    ring_arrive(2, 4)
    unpack(4)
    project(2, slice(None))
    offer(2)
    activate(1)
    activate(2)
    act_out[...] = jnp.dot(act_perm[...], perm[...], preferred_element_type=F32).astype(BF16)
    for copy in h_copies:
        copy.wait_recv()

    quarters = [lax.rem(x + 2, 4), lax.rem(x + 1, 4), lax.rem(x + 3, 4), x]
    g_copies = []

    def half(i, rows, which):
        columns = pl.ds(pl.multiple_of(quarters[i] * WINDOW + 384 * which, 128), 384)
        return jnp.dot(hidden[rows, :], gathered[:, columns], preferred_element_type=F32)

    def give(i, rows):
        g_send[i, rows, :] = half(i, rows, 1 - core).astype(BF16)
        n = len(g_copies)
        g_copies.append(launch(remote(
            g_send.at[i, rows], g_recv.at[i, rows], g_s.at[n], g_r.at[n], other_core)))

    def keep(i):
        g_own[i] = half(i, pl.ds(0, 3 * ROWS), core)

    def pair_sum(i, rows):
        return g_own[i, rows, :] + g_recv[i, rows, :].astype(F32)

    pieces = 3 * ROWS // PIECE
    sides = (x + 1, x + 3)
    far_copies, near_copies, mid_copies = {}, {}, {}

    def rows_at(p, part_of=None):
        if part_of is None:
            return pl.ds(p * PIECE, PIECE)
        return pl.ds(p * PIECE + part_of * (PIECE // 2), PIECE // 2)

    def send_far(p):
        x_far[rows_at(p), :] = pair_sum(0, rows_at(p)).astype(BF16)
        for way in (0, 1):
            far_copies[p, way] = launch(remote(
                x_far.at[rows_at(p, way)], x_mid.at[rows_at(p, way)],
                m_s.at[p, way], m_r.at[p, way], device(sides[way], y, z, core)))

    def send_near(p):
        for way in (0, 1):
            rows = rows_at(p, 1 - way)
            x_send[way, rows, :] = pair_sum(1 + way, rows).astype(BF16)
            near_copies[p, way] = launch(remote(
                x_send.at[way, rows], x_recv.at[way, rows],
                n_s.at[p, way], n_r.at[p, way], device(sides[way], y, z, core)))

    def send_mid(p):
        for way in (0, 1):
            rows = rows_at(p, way)
            far_copies[p, way].wait_recv()
            x_send[way, rows, :] = (pair_sum(1 + way, rows) + x_mid[rows, :].astype(F32)).astype(BF16)
            mid_copies[p, way] = launch(remote(
                x_send.at[way, rows], x_recv.at[way, rows],
                x_s.at[p, way], x_r.at[p, way], device(sides[way], y, z, core)))

    leaving = []

    def send_owner(p):
        for way in (0, 1):
            near_copies[p, way].wait_recv()
            mid_copies[p, way].wait_recv()
        rows = rows_at(p)
        z_send[rows, :] = (
            pair_sum(3, rows) + x_recv[0, rows, :].astype(F32) + x_recv[1, rows, :].astype(F32)
        ).astype(BF16)
        s, there = p * PIECE // ROWS, p * PIECE % ROWS
        for i in range(3):
            block = 5 * j + 3 * core + i
            owner, side = block // 2, lax.rem(block, 2)
            valid = jnp.logical_or(core == 0, j == 2) if i == 2 else True
            here = jnp.logical_and(owner == z_hi * 2 + core, j == s)
            src = z_send.at[rows, pl.ds(128 * i, 128)]
            dst = z_recv.at[z_hi, pl.ds(there, PIECE), pl.ds(pl.multiple_of(128 * side, 128), 128)]
            arrived = f_r.at[z_hi, side, there // PIECE]
            away = remote(
                src, dst, f_s.at[p, i], arrived, {"inter": x * 8 + owner, "intra": s * 8 + y})
            stay = pltpu.make_async_copy(src, dst, arrived)
            leaves = jnp.logical_and(valid, jnp.logical_not(here))

            @pl.when(leaves)
            def _():
                away.start()

            @pl.when(jnp.logical_and(valid, here))
            def _():
                stay.start()

            leaving.append((leaves, away))

    every = pl.ds(0, 3 * ROWS)
    give(0, pl.ds(0, 288))
    give(0, pl.ds(288, 288))
    keep(0)
    give(1, every)
    give(2, every)
    g_copies[0].wait_recv()
    send_far(0)
    send_far(1)
    keep(1)
    keep(2)
    g_copies[1].wait_recv()
    g_copies[2].wait_recv()
    g_copies[3].wait_recv()
    send_near(0)
    send_near(1)
    give(3, every)
    send_mid(0)
    send_mid(1)
    send_far(2)
    send_far(3)
    send_near(2)
    keep(3)
    g_copies[4].wait_recv()
    send_owner(0)
    send_near(3)
    send_mid(2)
    send_owner(1)
    send_mid(3)
    send_far(4)
    send_far(5)
    send_near(4)
    send_owner(2)
    send_near(5)
    send_mid(4)
    send_owner(3)
    send_mid(5)
    send_owner(4)
    send_owner(5)

    for copy in pending + leaving_to[0] + leaving_to[1]:
        copy.wait_send()
    for leaves, copy in leaving:
        @pl.when(leaves)
        def _():
            copy.wait_send()

    total = None
    for source in range(4):
        for side in range(2):
            for part_of in range(ROWS // PIECE):
                piece = z_recv.at[source, pl.ds(PIECE * part_of, PIECE), pl.ds(128 * side, 128)]
                pltpu.make_async_copy(piece, piece, f_r.at[source, side, part_of]).wait()
        value = z_recv[source].astype(F32)
        total = value if total is None else total + value
    grad_out[...] = total


def per_device(tokens, weight_codes, exponents, upstream):
    vmem = pl.BlockSpec(memory_space=pltpu.VMEM)
    hbm = pl.BlockSpec(memory_space=pltpu.HBM)
    dma = pltpu.SemaphoreType.DMA
    pieces = 3 * ROWS // PIECE
    return pl.pallas_call(
        kernel,
        out_shape=(
            jax.ShapeDtypeStruct((ROWS, 456), BF16),
            jax.ShapeDtypeStruct((ROWS, 256), F32),
        ),
        in_specs=[hbm] * 4,
        out_specs=(vmem, vmem),
        scratch_shapes=[
            pltpu.VMEM((19, 8192), BF16),
            pltpu.VMEM((19, 64), jnp.int32),
            pltpu.VMEM((ROWS, 456), BF16),
            pltpu.VMEM((3, 16, UNIT), BF16),
            pltpu.VMEM((3, 16, PACK), F32),
            pltpu.VMEM((512, UNIT), BF16),
            pltpu.VMEM((3 * ROWS, WIDTH), BF16),
            pltpu.VMEM((512, 456), BF16),
            pltpu.VMEM((ROWS, 512), F32),
            pltpu.VMEM((3 * ROWS, 512), F32),
            pltpu.VMEM((2, ROWS, 512), BF16),
            pltpu.VMEM((2, ROWS, 512), BF16),
            pltpu.VMEM((ROWS, 512), BF16),
            pltpu.VMEM((3 * ROWS, 512), BF16),
            pltpu.VMEM((4, 3 * ROWS, 384), BF16),
            pltpu.VMEM((4, 3 * ROWS, 384), BF16),
            pltpu.VMEM((4, 3 * ROWS, 384), F32),
            pltpu.VMEM((3 * ROWS, 384), BF16),
            pltpu.VMEM((2, 3 * ROWS, 384), BF16),
            pltpu.VMEM((3 * ROWS, 384), BF16),
            pltpu.VMEM((2, 3 * ROWS, 384), BF16),
            pltpu.VMEM((3 * ROWS, 384), BF16),
            pltpu.VMEM((4, ROWS, 256), BF16),
            dma((3,)), dma((4,)),
            dma((2,)), dma((2,)),
            dma((3, 2, 4)), dma((3, 2, 4)),
            dma((2, 4)), dma((2, 4)),
            dma((2, 4)), dma((2, 4)),
            dma((2, 4)), dma((2, 4)),
            dma((3, 2)), dma((3, 2)),
            dma((3, 2)), dma((3, 2)),
            dma((5,)), dma((5,)),
            dma((pieces, 2)), dma((pieces, 2)),
            dma((pieces, 2)), dma((pieces, 2)),
            dma((pieces, 2)), dma((pieces, 2)),
            dma((pieces, 3)), dma((4, 2, ROWS // PIECE)),
        ],
        compiler_params=pltpu.CompilerParams(
            collective_id=0, has_side_effects=True, vmem_limit_bytes=107 << 19),
        cost_estimate=pl.CostEstimate(
            flops=4 * ROWS * 8192 * 456, bytes_accessed=8 << 20, transcendentals=ROWS * 512),
    )(tokens, weight_codes, exponents, upstream)


def solution(mesh):
    placed = (
        P("intra", None),
        P(("inter", "intra"), None),
        P(("inter", "intra"), None),
        P("intra", "inter"),
    )
    return jax.shard_map(
        per_device,
        mesh=mesh,
        in_specs=placed,
        out_specs=(P("intra", "inter"), P("intra", "inter")),
        check_vma=False,
    )
```

```python
import jax
import jax.numpy as jnp
from jax import lax
from jax.experimental import pallas as pl
from jax.experimental.pallas import tpu as pltpu
from jax.sharding import PartitionSpec as P

MESH = pl.DeviceIdType.MESH
F32 = jnp.float32
BF16 = jnp.bfloat16

WINDOW = 768
WIDTH = 4 * WINDOW
ROWS = 192
SLOT = 64
PACK = 640
UNIT = WIDTH + PACK
AHEAD = 2
PIECE = 96
CHUNKS = ((0, 256), (256, 128), (384, 128))
NT = (((1,), (1,)), ((), ()))


def slot_of(offset):
    if offset == 0:
        return 0
    return 2 * offset - 1 if offset > 0 else -2 * offset


def device(x, y, z, core):
    x, y, z, core = lax.rem(x + 8, 4), lax.rem(y + 8, 8), lax.rem(z + 24, 12), lax.rem(core + 2, 2)
    return {"inter": x * 8 + (z // 3) * 2 + core, "intra": lax.rem(z, 3) * 8 + y}


def kernel(
    tokens, codes_hbm, exponents_hbm, upstream_hbm, act_out, grad_out,
    codes, exponents, upstream,
    windows, packed, gathered, tok, perm, up_perm, p_part, p_send, p_recv, act_perm, hidden,
    g_send, g_recv, g_own, x_far, x_send, x_mid, x_recv, z_send, z_recv,
    end_sem, round_sem, load_sem, tok_own_sem, a2a_s, a2a_r, ring_s, ring_r, tok_s, tok_r, tokx_s, tokx_r, tokc_s, tokc_r,
    p_s, p_r, h_s, h_r, g_s, g_r, m_s, m_r, n_s, n_r, x_s, x_r, f_s, f_r,
):
    inter = lax.axis_index("inter")
    intra = lax.axis_index("intra")
    x, z_hi, core = inter // 8, lax.rem(inter // 2, 4), lax.rem(inter, 2)
    j, y = intra // 8, lax.rem(intra, 8)
    z = z_hi * 3 + j
    other_core = device(x, y, z, core + 1)

    def part(m):
        return lax.rem(j + m, 3)

    def group_peer(m):
        return {"inter": inter, "intra": part(m) * 8 + y}

    def rows_of(s, size=ROWS, start=0):
        return pl.ds(pl.multiple_of(s * ROWS + start, 16), size)

    def remote(src, dst, send_sem, recv_sem, to):
        return pltpu.make_async_remote_copy(
            src_ref=src, dst_ref=dst, send_sem=send_sem, recv_sem=recv_sem,
            device_id=to, device_id_type=MESH,
        )

    pending = []

    def launch(copy):
        copy.start()
        pending.append(copy)
        return copy

    loads = [
        pltpu.make_async_copy(src, dst, load_sem.at[i])
        for i, (src, dst) in enumerate(
            ((codes_hbm, codes), (exponents_hbm, exponents), (upstream_hbm, upstream)))
    ]
    for copy in loads:
        copy.start()

    barrier = pltpu.get_barrier_semaphore()
    peers = [other_core, group_peer(1), group_peer(2)]
    peers += [device(x, y + 1, z, core), device(x, y + 7, z, core)]
    peers += [device(x + 1, y, z, core), device(x + 3, y, z, core)]
    below = [device(x, y, z + 11, core), device(x, y, z + 11, core + 1)]
    above = [device(x, y, z + 1, core), device(x, y, z + 1, core + 1)]

    def greet(semaphore, devices):
        for peer in devices:
            pl.semaphore_signal(semaphore, inc=1, device_id=peer, device_id_type=MESH)

    greet(barrier, peers + below)

    @pl.when(z != 11)
    def _():
        greet(barrier, above)

    def token_columns(q, to_part):
        return pl.ds(pl.multiple_of(q * 2048 + to_part * 640, 128), WINDOW)

    own_copies = [
        pltpu.make_async_copy(
            tokens.at[:, token_columns(q, j)],
            tok.at[rows_of(j), pl.ds(q * WINDOW, WINDOW)],
            tok_own_sem.at[q],
        )
        for q in range(4)
    ]
    for copy in own_copies:
        copy.start()

    packed[...] = jnp.zeros_like(packed)
    loads[0].wait()
    loads[1].wait()
    scale = jnp.exp2(exponents[...].astype(F32)).astype(BF16).astype(F32)
    blank = jnp.zeros((16, 128), BF16)
    for q in range(4):
        for i in range(16):
            b = q * 16 + i
            value = codes[:, b * 128:(b + 1) * 128].astype(F32) * scale[:, b:b + 1]
            to = min(i // 5, 2)
            at = q * 6 + i - 5 * to
            windows[to, :, at * 128:(at + 1) * 128] = value[0:16].astype(BF16)
            run, lane = 3 * (at // 5), at % 5 * 128
            packed[to, run:run + 3, lane:lane + 128] = value[16:19]
        for to in range(2):
            windows[to, :, q * WINDOW + 640:(q + 1) * WINDOW] = blank
    for to in range(3):
        windows[to, :, WIDTH:] = packed[to].astype(BF16)
    mine = pl.ds(pl.multiple_of(16 * j, 16), 16)
    gathered[mine, :] = windows[j]

    pl.semaphore_wait(barrier, jnp.where(z == 0, len(peers) + 2, len(peers) + 4))

    @pl.when(z == 11)
    def _():
        greet(end_sem, above)

    a2a = [
        launch(remote(
            windows.at[part(m)], gathered.at[mine], a2a_s.at[m - 1], a2a_r.at[m - 1], group_peer(m)))
        for m in (1, 2)
    ]

    def unit_rows(u, slot):
        return pl.ds(pl.multiple_of(slot * SLOT + 16 * part(u), 16), 16)

    def ring(u, way, k):
        sign = 1 if way == 0 else -1
        return remote(
            gathered.at[unit_rows(u, slot_of(sign * (k - 1)))],
            gathered.at[unit_rows(u, slot_of(sign * k))],
            ring_s.at[u, way, k - 1], ring_r.at[u, way, k - 1], device(x, y + sign, z, core))

    def ring_last(u):
        odd = lax.rem(core + u, 2)
        return remote(
            gathered.at[unit_rows(u, slot_of(3) + odd)], gathered.at[unit_rows(u, slot_of(4))],
            ring_s.at[u, 0, 3], ring_r.at[u, 0, 3], device(x, y + 1 - 2 * odd, z, core))

    leaving_to = ([], [])

    def ring_launch(copy, ways):
        for way in ways:
            if len(leaving_to[way]) >= AHEAD:
                leaving_to[way].pop(0).wait_send()
            leaving_to[way].append(copy)
        copy.start()

    def ring_open(u):
        for way in (0, 1):
            ring_launch(ring(u, way, 1), (way,))

    def ring_arrive(u, k):
        if k == 4:
            ring_last(u).wait_recv()
            return
        for way in (0, 1):
            ring(u, way, k).wait_recv()
            if k < 3:
                ring_launch(ring(u, way, k + 1), (way,))
        if k == 3:
            launch(ring_last(u))

    ring_open(0)

    at = lax.broadcasted_iota(jnp.int32, (512, 456), 0)
    natural = lax.broadcasted_iota(jnp.int32, (512, 456), 1)
    slot, within = at >> 6, at & 63
    offset = jnp.where((slot & 1) == 1, (slot + 1) >> 1, -(slot >> 1))
    source_y = (y - offset + 8) & 7
    late = within - 48
    late_z = (late >= 3).astype(jnp.int32) + (late >= 6).astype(jnp.int32)
    source_z = jnp.where(late < 0, within >> 4, late_z)
    source_row = jnp.where(late < 0, within & 15, 16 + late - 3 * late_z)
    matches = (natural == (source_z * 8 + source_y) * 19 + source_row) & (late < 9)
    perm[...] = jnp.where(matches, 1.0, 0.0).astype(BF16)
    loads[2].wait()
    up_perm[...] = lax.dot_general(upstream[...], perm[...], NT, preferred_element_type=F32)

    to_row = lax.broadcasted_iota(jnp.int32, (80, 48), 0)
    from_row = lax.broadcasted_iota(jnp.int32, (80, 48), 1)
    run, within = to_row >> 4, to_row & 15
    late_z = (within >= 3).astype(jnp.int32) + (within >= 6).astype(jnp.int32)
    matches = (from_row == 16 * late_z + 3 * run + within - 3 * late_z) & (within < 9)
    unpacker = jnp.where(matches, 1.0, 0.0).astype(BF16)

    def unpack(offset):
        top = slot_of(offset) * SLOT
        rows = jnp.dot(unpacker, gathered[top:top + 48, WIDTH:], preferred_element_type=F32).astype(BF16)
        for c in range(5):
            width = min(PACK, WIDTH - c * PACK)
            gathered[top + 48:top + 64, c * PACK:c * PACK + width] = rows[16 * c:16 * c + 16, :width]

    quarter = 96 * core + 48 * lax.rem(x, 2)
    token_copies, side_copies, core_copies = {}, {}, {}

    def tokens_to(way, q, to, semaphores):
        return remote(
            tokens.at[
                pl.ds(pl.multiple_of(quarter, 16), 48), token_columns(q, part(1 + way))],
            tok.at[rows_of(j, 48, quarter), pl.ds(q * WINDOW, WINDOW)],
            semaphores.at[q], tok_r.at[way, q], to)

    token_again = []
    for q in range(4):
        token_copies[0, q] = tokens_to(0, q, device(x, y, z + 1, core), tok_s.at[0])
        token_copies[1, q] = tokens_to(1, q, device(x, y, z + 11, core), tok_s.at[1])
        token_again.append(tokens_to(0, q, device(x, y, z + 10, core), tok_s.at[2]))
    token_sends = (
        (z != 11, [token_copies[0, q] for q in range(4)]),
        (z == 2, token_again),
        (z != 0, [token_copies[1, q] for q in range(4)]),
        (z == 0, [token_copies[1, q] for q in range(4)]),
    )

    def tokens_send(n):
        condition, copies = token_sends[n]

        @pl.when(condition)
        def _():
            for copy in copies:
                copy.start()

    def tokens_aside(q):
        for way, step in ((0, 1), (1, 3)):
            token_copies[way, q].wait_recv()
            block = tok.at[rows_of(part(2 - way), 48, quarter), pl.ds(q * WINDOW, WINDOW)]
            side_copies[way, q] = launch(remote(
                block, block, tokx_s.at[way, q], tokx_r.at[way, q], device(x + step, y, z, core)))

    def tokens_across(q):
        for way in (0, 1):
            side_copies[way, q].wait_recv()
            block = tok.at[rows_of(part(2 - way), 96, 96 * core), pl.ds(q * WINDOW, WINDOW)]
            core_copies[way, q] = launch(remote(
                block, block, tokc_s.at[way, q], tokc_r.at[way, q], other_core))

    def project(c, rows):
        start, width = CHUNKS[c]
        p_part[rows, pl.ds(start, width)] = lax.dot_general(
            tok[rows, :], gathered[start:start + width, :WIDTH], NT, preferred_element_type=F32)

    def offer(c):
        columns = pl.ds(*CHUNKS[c])
        for m in (1, 2):
            p_send[m - 1, :, columns] = p_part[rows_of(part(m)), columns].astype(BF16)
            p_copies[c, m] = launch(remote(
                p_send.at[m - 1, :, columns], p_recv.at[m - 1, :, columns],
                p_s.at[c, m - 1], p_r.at[c, m - 1], group_peer(m)))

    def activate(c):
        columns = pl.ds(*CHUNKS[c])
        for m in (1, 2):
            p_copies[c, m].wait_recv()
        projected = p_part[rows_of(j), columns] + p_recv[0, :, columns].astype(F32) + p_recv[1, :, columns].astype(F32)
        sig = 1.0 / (1.0 + jnp.exp(-projected))
        slope = sig * (1.0 + projected * (1.0 - sig))
        hidden[rows_of(j), columns] = (up_perm[:, columns] * slope).astype(BF16)
        block = hidden.at[rows_of(j), columns]
        for m in (1, 2):
            h_copies.append(launch(remote(
                block, block, h_s.at[c, m - 1], h_r.at[c, m - 1], group_peer(m))))
        act_perm[:, columns] = (projected * sig).astype(BF16)

    p_copies, h_copies = {}, []

    ring_arrive(0, 1)
    for u in (1, 2):
        a2a[2 - u].wait_recv()
        ring_open(u)
    def tell(n):
        step = 1 if n == 0 else 2
        greet(round_sem.at[n], [device(x, y, z + step, core), device(x, y, z + 12 - step, core)])

    def hear(n):
        pl.semaphore_wait(round_sem.at[n], 2)

    for n in (0, 2, 1):
        tokens_send(n)
    unpack(0)
    ring_arrive(0, 2)
    tokens_aside(0)
    ring_arrive(1, 1)
    tokens_aside(1)
    ring_arrive(2, 1)

    @pl.when(z == 0)
    def _():
        pl.semaphore_wait(end_sem, 2)

    tokens_send(3)
    tell(0)
    tokens_aside(2)
    unpack(1)
    unpack(-1)
    tokens_aside(3)
    tokens_across(0)
    ring_arrive(0, 3)
    tokens_across(1)
    tokens_across(2)
    ring_arrive(1, 2)
    tokens_across(3)
    ring_arrive(2, 2)
    unpack(2)
    unpack(-2)
    for copy in own_copies:
        copy.wait()
    project(0, rows_of(j))
    ring_arrive(0, 4)
    for copy in core_copies.values():
        copy.wait_recv()
    project(0, rows_of(part(1)))
    project(0, rows_of(part(2)))
    offer(0)
    ring_arrive(1, 3)
    ring_arrive(2, 3)
    hear(0)
    tell(1)
    unpack(3)
    unpack(-3)
    project(1, slice(None))
    offer(1)
    activate(0)
    ring_arrive(1, 4)
    ring_arrive(2, 4)
    hear(1)
    tell(2)
    unpack(4)
    project(2, slice(None))
    offer(2)
    activate(1)
    activate(2)
    act_out[...] = jnp.dot(act_perm[...], perm[...], preferred_element_type=F32).astype(BF16)
    for copy in h_copies:
        copy.wait_recv()

    quarters = [lax.rem(x + 2, 4), lax.rem(x + 1, 4), lax.rem(x + 3, 4), x]
    g_copies = []

    def half(i, rows, which):
        columns = pl.ds(pl.multiple_of(quarters[i] * WINDOW + 384 * which, 128), 384)
        return jnp.dot(hidden[rows, :], gathered[:, columns], preferred_element_type=F32)

    def give(i, rows):
        g_send[i, rows, :] = half(i, rows, 1 - core).astype(BF16)
        n = len(g_copies)
        g_copies.append(launch(remote(
            g_send.at[i, rows], g_recv.at[i, rows], g_s.at[n], g_r.at[n], other_core)))

    def keep(i):
        g_own[i] = half(i, pl.ds(0, 3 * ROWS), core)

    def pair_sum(i, rows):
        return g_own[i, rows, :] + g_recv[i, rows, :].astype(F32)

    pieces = 3 * ROWS // PIECE
    sides = (x + 1, x + 3)
    far_copies, near_copies, mid_copies = {}, {}, {}

    def rows_at(p, part_of=None):
        if part_of is None:
            return pl.ds(p * PIECE, PIECE)
        return pl.ds(p * PIECE + part_of * (PIECE // 2), PIECE // 2)

    def send_far(p):
        x_far[rows_at(p), :] = pair_sum(0, rows_at(p)).astype(BF16)
        for way in (0, 1):
            far_copies[p, way] = launch(remote(
                x_far.at[rows_at(p, way)], x_mid.at[rows_at(p, way)],
                m_s.at[p, way], m_r.at[p, way], device(sides[way], y, z, core)))

    def send_near(p):
        for way in (0, 1):
            rows = rows_at(p, 1 - way)
            x_send[way, rows, :] = pair_sum(1 + way, rows).astype(BF16)
            near_copies[p, way] = launch(remote(
                x_send.at[way, rows], x_recv.at[way, rows],
                n_s.at[p, way], n_r.at[p, way], device(sides[way], y, z, core)))

    def send_mid(p):
        for way in (0, 1):
            rows = rows_at(p, way)
            far_copies[p, way].wait_recv()
            x_send[way, rows, :] = (pair_sum(1 + way, rows) + x_mid[rows, :].astype(F32)).astype(BF16)
            mid_copies[p, way] = launch(remote(
                x_send.at[way, rows], x_recv.at[way, rows],
                x_s.at[p, way], x_r.at[p, way], device(sides[way], y, z, core)))

    leaving = []

    def send_owner(p):
        for way in (0, 1):
            near_copies[p, way].wait_recv()
            mid_copies[p, way].wait_recv()
        rows = rows_at(p)
        z_send[rows, :] = (
            pair_sum(3, rows) + x_recv[0, rows, :].astype(F32) + x_recv[1, rows, :].astype(F32)
        ).astype(BF16)
        s, there = p * PIECE // ROWS, p * PIECE % ROWS
        for i in range(3):
            block = 5 * j + 3 * core + i
            owner, side = block // 2, lax.rem(block, 2)
            valid = jnp.logical_or(core == 0, j == 2) if i == 2 else True
            here = jnp.logical_and(owner == z_hi * 2 + core, j == s)
            src = z_send.at[rows, pl.ds(128 * i, 128)]
            dst = z_recv.at[z_hi, pl.ds(there, PIECE), pl.ds(pl.multiple_of(128 * side, 128), 128)]
            arrived = f_r.at[z_hi, side, there // PIECE]
            away = remote(
                src, dst, f_s.at[p, i], arrived, {"inter": x * 8 + owner, "intra": s * 8 + y})
            stay = pltpu.make_async_copy(src, dst, arrived)
            leaves = jnp.logical_and(valid, jnp.logical_not(here))

            @pl.when(leaves)
            def _():
                away.start()

            @pl.when(jnp.logical_and(valid, here))
            def _():
                stay.start()

            leaving.append((leaves, away))

    every = pl.ds(0, 3 * ROWS)
    give(0, pl.ds(0, 288))
    give(0, pl.ds(288, 288))
    keep(0)
    give(1, every)
    give(2, every)
    g_copies[0].wait_recv()
    send_far(0)
    send_far(1)
    keep(1)
    keep(2)
    g_copies[1].wait_recv()
    g_copies[2].wait_recv()
    g_copies[3].wait_recv()
    send_near(0)
    send_near(1)
    give(3, every)
    send_mid(0)
    send_mid(1)
    send_far(2)
    send_far(3)
    send_near(2)
    keep(3)
    g_copies[4].wait_recv()
    hear(2)
    send_owner(0)
    send_near(3)
    send_mid(2)
    send_owner(1)
    send_mid(3)
    send_far(4)
    send_far(5)
    send_near(4)
    send_owner(2)
    send_near(5)
    send_mid(4)
    send_owner(3)
    send_mid(5)
    send_owner(4)
    send_owner(5)

    for copy in pending + leaving_to[0] + leaving_to[1]:
        copy.wait_send()
    for condition, copies in token_sends:
        @pl.when(condition)
        def _():
            for copy in copies:
                copy.wait_send()
    for leaves, copy in leaving:
        @pl.when(leaves)
        def _():
            copy.wait_send()

    total = None
    for source in range(4):
        for side in range(2):
            for part_of in range(ROWS // PIECE):
                piece = z_recv.at[source, pl.ds(PIECE * part_of, PIECE), pl.ds(128 * side, 128)]
                pltpu.make_async_copy(piece, piece, f_r.at[source, side, part_of]).wait()
        value = z_recv[source].astype(F32)
        total = value if total is None else total + value
    grad_out[...] = total


def per_device(tokens, weight_codes, exponents, upstream):
    vmem = pl.BlockSpec(memory_space=pltpu.VMEM)
    hbm = pl.BlockSpec(memory_space=pltpu.HBM)
    dma = pltpu.SemaphoreType.DMA
    pieces = 3 * ROWS // PIECE
    return pl.pallas_call(
        kernel,
        out_shape=(
            jax.ShapeDtypeStruct((ROWS, 456), BF16),
            jax.ShapeDtypeStruct((ROWS, 256), F32),
        ),
        in_specs=[hbm] * 4,
        out_specs=(vmem, vmem),
        scratch_shapes=[
            pltpu.VMEM((19, 8192), BF16),
            pltpu.VMEM((19, 64), jnp.int32),
            pltpu.VMEM((ROWS, 456), BF16),
            pltpu.VMEM((3, 16, UNIT), BF16),
            pltpu.VMEM((3, 16, PACK), F32),
            pltpu.VMEM((512, UNIT), BF16),
            pltpu.VMEM((3 * ROWS, WIDTH), BF16),
            pltpu.VMEM((512, 456), BF16),
            pltpu.VMEM((ROWS, 512), F32),
            pltpu.VMEM((3 * ROWS, 512), F32),
            pltpu.VMEM((2, ROWS, 512), BF16),
            pltpu.VMEM((2, ROWS, 512), BF16),
            pltpu.VMEM((ROWS, 512), BF16),
            pltpu.VMEM((3 * ROWS, 512), BF16),
            pltpu.VMEM((4, 3 * ROWS, 384), BF16),
            pltpu.VMEM((4, 3 * ROWS, 384), BF16),
            pltpu.VMEM((4, 3 * ROWS, 384), F32),
            pltpu.VMEM((3 * ROWS, 384), BF16),
            pltpu.VMEM((2, 3 * ROWS, 384), BF16),
            pltpu.VMEM((3 * ROWS, 384), BF16),
            pltpu.VMEM((2, 3 * ROWS, 384), BF16),
            pltpu.VMEM((3 * ROWS, 384), BF16),
            pltpu.VMEM((4, ROWS, 256), BF16),
            pltpu.SemaphoreType.REGULAR, pltpu.SemaphoreType.REGULAR((3,)),
            dma((3,)), dma((4,)),
            dma((2,)), dma((2,)),
            dma((3, 2, 4)), dma((3, 2, 4)),
            dma((3, 4)), dma((2, 4)),
            dma((2, 4)), dma((2, 4)),
            dma((2, 4)), dma((2, 4)),
            dma((3, 2)), dma((3, 2)),
            dma((3, 2)), dma((3, 2)),
            dma((5,)), dma((5,)),
            dma((pieces, 2)), dma((pieces, 2)),
            dma((pieces, 2)), dma((pieces, 2)),
            dma((pieces, 2)), dma((pieces, 2)),
            dma((pieces, 3)), dma((4, 2, ROWS // PIECE)),
        ],
        compiler_params=pltpu.CompilerParams(
            collective_id=0, has_side_effects=True, vmem_limit_bytes=107 << 19),
        cost_estimate=pl.CostEstimate(
            flops=4 * ROWS * 8192 * 456, bytes_accessed=8 << 20, transcendentals=ROWS * 512),
    )(tokens, weight_codes, exponents, upstream)


def solution(mesh):
    placed = (
        P("intra", None),
        P(("inter", "intra"), None),
        P(("inter", "intra"), None),
        P("intra", "inter"),
    )
    return jax.shard_map(
        per_device,
        mesh=mesh,
        in_specs=placed,
        out_specs=(P("intra", "inter"), P("intra", "inter")),
        check_vma=False,
    )
```

```python
import jax
import jax.numpy as jnp
from jax import lax
from jax.experimental import pallas as pl
from jax.experimental.pallas import tpu as pltpu
from jax.sharding import PartitionSpec as P

MESH = pl.DeviceIdType.MESH
F32 = jnp.float32
BF16 = jnp.bfloat16

WINDOW = 768
WIDTH = 4 * WINDOW
ROWS = 192
SLOT = 64
PACK = 640
UNIT = WIDTH + PACK
AHEAD = 2
PIECE = 96
CHUNKS = ((0, 256), (256, 128), (384, 128))
NT = (((1,), (1,)), ((), ()))


def slot_of(offset):
    if offset == 0:
        return 0
    return 2 * offset - 1 if offset > 0 else -2 * offset


def device(x, y, z, core):
    x, y, z, core = lax.rem(x + 8, 4), lax.rem(y + 8, 8), lax.rem(z + 24, 12), lax.rem(core + 2, 2)
    return {"inter": x * 8 + (z // 3) * 2 + core, "intra": lax.rem(z, 3) * 8 + y}


def kernel(
    tokens, codes_hbm, exponents_hbm, upstream_hbm, act_out, grad_out,
    codes, exponents, upstream,
    windows, packed, gathered, tok, perm, up_perm, p_part, p_send, p_recv, act_perm, hidden,
    g_send, g_recv, g_own, x_far, x_send, x_mid, x_recv, z_send, z_recv,
    end_sem, round_sem, load_sem, tok_own_sem, a2a_s, a2a_r, ring_s, ring_r, tok_s, tok_r, tokx_s, tokx_r, tokc_s, tokc_r,
    p_s, p_r, h_s, h_r, g_s, g_r, m_s, m_r, n_s, n_r, x_s, x_r, f_s, f_r,
):
    inter = lax.axis_index("inter")
    intra = lax.axis_index("intra")
    x, z_hi, core = inter // 8, lax.rem(inter // 2, 4), lax.rem(inter, 2)
    j, y = intra // 8, lax.rem(intra, 8)
    z = z_hi * 3 + j
    other_core = device(x, y, z, core + 1)

    def part(m):
        return lax.rem(j + m, 3)

    def group_peer(m):
        return {"inter": inter, "intra": part(m) * 8 + y}

    def rows_of(s, size=ROWS, start=0):
        return pl.ds(pl.multiple_of(s * ROWS + start, 16), size)

    def remote(src, dst, send_sem, recv_sem, to):
        return pltpu.make_async_remote_copy(
            src_ref=src, dst_ref=dst, send_sem=send_sem, recv_sem=recv_sem,
            device_id=to, device_id_type=MESH,
        )

    pending = []

    def launch(copy):
        copy.start()
        pending.append(copy)
        return copy

    loads = [
        pltpu.make_async_copy(src, dst, load_sem.at[i])
        for i, (src, dst) in enumerate(
            ((codes_hbm, codes), (exponents_hbm, exponents), (upstream_hbm, upstream)))
    ]
    for copy in loads:
        copy.start()

    barrier = pltpu.get_barrier_semaphore()
    peers = [other_core, group_peer(1), group_peer(2)]
    peers += [device(x, y + 1, z, core), device(x, y + 7, z, core)]
    peers += [device(x + 1, y, z, core), device(x + 3, y, z, core)]
    below = [device(x, y, z + 11, core), device(x, y, z + 11, core + 1)]
    above = [device(x, y, z + 1, core), device(x, y, z + 1, core + 1)]

    def greet(semaphore, devices):
        for peer in devices:
            pl.semaphore_signal(semaphore, inc=1, device_id=peer, device_id_type=MESH)

    greet(barrier, peers + below)

    @pl.when(z != 11)
    def _():
        greet(barrier, above)

    def token_columns(q, to_part):
        return pl.ds(pl.multiple_of(q * 2048 + to_part * 640, 128), WINDOW)

    own_copies = [
        pltpu.make_async_copy(
            tokens.at[:, token_columns(q, j)],
            tok.at[rows_of(j), pl.ds(q * WINDOW, WINDOW)],
            tok_own_sem.at[q],
        )
        for q in range(4)
    ]
    for copy in own_copies:
        copy.start()

    packed[...] = jnp.zeros_like(packed)
    loads[0].wait()
    loads[1].wait()
    scale = jnp.exp2(exponents[...].astype(F32)).astype(BF16).astype(F32)
    blank = jnp.zeros((16, 128), BF16)
    for q in range(4):
        for i in range(16):
            b = q * 16 + i
            value = codes[:, b * 128:(b + 1) * 128].astype(F32) * scale[:, b:b + 1]
            to = min(i // 5, 2)
            at = q * 6 + i - 5 * to
            windows[to, :, at * 128:(at + 1) * 128] = value[0:16].astype(BF16)
            run, lane = 3 * (at // 5), at % 5 * 128
            packed[to, run:run + 3, lane:lane + 128] = value[16:19]
        for to in range(2):
            windows[to, :, q * WINDOW + 640:(q + 1) * WINDOW] = blank
    for to in range(3):
        windows[to, :, WIDTH:] = packed[to].astype(BF16)
    mine = pl.ds(pl.multiple_of(16 * j, 16), 16)
    gathered[mine, :] = windows[j]

    pl.semaphore_wait(barrier, jnp.where(z == 0, len(peers) + 2, len(peers) + 4))

    @pl.when(z == 11)
    def _():
        greet(end_sem, above)

    a2a = [
        launch(remote(
            windows.at[part(m)], gathered.at[mine], a2a_s.at[m - 1], a2a_r.at[m - 1], group_peer(m)))
        for m in (1, 2)
    ]

    def unit_rows(u, slot):
        return pl.ds(pl.multiple_of(slot * SLOT + 16 * part(u), 16), 16)

    def ring(u, way, k):
        sign = 1 if way == 0 else -1
        return remote(
            gathered.at[unit_rows(u, slot_of(sign * (k - 1)))],
            gathered.at[unit_rows(u, slot_of(sign * k))],
            ring_s.at[u, way, k - 1], ring_r.at[u, way, k - 1], device(x, y + sign, z, core))

    def ring_last(u):
        odd = lax.rem(core + u, 2)
        return remote(
            gathered.at[unit_rows(u, slot_of(3) + odd)], gathered.at[unit_rows(u, slot_of(4))],
            ring_s.at[u, 0, 3], ring_r.at[u, 0, 3], device(x, y + 1 - 2 * odd, z, core))

    leaving_to = ([], [])

    def ring_launch(copy, ways):
        for way in ways:
            if len(leaving_to[way]) >= AHEAD:
                leaving_to[way].pop(0).wait_send()
            leaving_to[way].append(copy)
        copy.start()

    def ring_open(u):
        for way in (0, 1):
            ring_launch(ring(u, way, 1), (way,))

    def ring_arrive(u, k):
        if k == 4:
            ring_last(u).wait_recv()
            return
        for way in (0, 1):
            ring(u, way, k).wait_recv()
            if k < 3:
                ring_launch(ring(u, way, k + 1), (way,))
        if k == 3:
            launch(ring_last(u))

    ring_open(0)

    at = lax.broadcasted_iota(jnp.int32, (512, 456), 0)
    natural = lax.broadcasted_iota(jnp.int32, (512, 456), 1)
    slot, within = at >> 6, at & 63
    offset = jnp.where((slot & 1) == 1, (slot + 1) >> 1, -(slot >> 1))
    source_y = (y - offset + 8) & 7
    late = within - 48
    late_z = (late >= 3).astype(jnp.int32) + (late >= 6).astype(jnp.int32)
    source_z = jnp.where(late < 0, within >> 4, late_z)
    source_row = jnp.where(late < 0, within & 15, 16 + late - 3 * late_z)
    matches = (natural == (source_z * 8 + source_y) * 19 + source_row) & (late < 9)
    perm[...] = jnp.where(matches, 1.0, 0.0).astype(BF16)
    loads[2].wait()
    up_perm[...] = lax.dot_general(upstream[...], perm[...], NT, preferred_element_type=F32)

    to_row = lax.broadcasted_iota(jnp.int32, (80, 48), 0)
    from_row = lax.broadcasted_iota(jnp.int32, (80, 48), 1)
    run, within = to_row >> 4, to_row & 15
    late_z = (within >= 3).astype(jnp.int32) + (within >= 6).astype(jnp.int32)
    matches = (from_row == 16 * late_z + 3 * run + within - 3 * late_z) & (within < 9)
    unpacker = jnp.where(matches, 1.0, 0.0).astype(BF16)

    def unpack(offset):
        top = slot_of(offset) * SLOT
        rows = jnp.dot(unpacker, gathered[top:top + 48, WIDTH:], preferred_element_type=F32).astype(BF16)
        for c in range(5):
            width = min(PACK, WIDTH - c * PACK)
            gathered[top + 48:top + 64, c * PACK:c * PACK + width] = rows[16 * c:16 * c + 16, :width]

    quarter = 96 * core + 48 * lax.rem(x, 2)
    token_copies, side_copies, core_copies = {}, {}, {}

    def tokens_to(way, q, to, semaphores):
        return remote(
            tokens.at[
                pl.ds(pl.multiple_of(quarter, 16), 48), token_columns(q, part(1 + way))],
            tok.at[rows_of(j, 48, quarter), pl.ds(q * WINDOW, WINDOW)],
            semaphores.at[q], tok_r.at[way, q], to)

    token_again = []
    for q in range(4):
        token_copies[0, q] = tokens_to(0, q, device(x, y, z + 1, core), tok_s.at[0])
        token_copies[1, q] = tokens_to(1, q, device(x, y, z + 11, core), tok_s.at[1])
        token_again.append(tokens_to(0, q, device(x, y, z + 10, core), tok_s.at[2]))
    token_sends = (
        (z != 11, [token_copies[0, q] for q in range(4)]),
        (z == 2, token_again),
        (z != 0, [token_copies[1, q] for q in range(4)]),
        (z == 0, [token_copies[1, q] for q in range(4)]),
    )

    def tokens_send(n):
        condition, copies = token_sends[n]

        @pl.when(condition)
        def _():
            for copy in copies:
                copy.start()

    def tokens_aside(q):
        for way, step in ((0, 1), (1, 3)):
            token_copies[way, q].wait_recv()
            block = tok.at[rows_of(part(2 - way), 48, quarter), pl.ds(q * WINDOW, WINDOW)]
            side_copies[way, q] = launch(remote(
                block, block, tokx_s.at[way, q], tokx_r.at[way, q], device(x + step, y, z, core)))

    def tokens_across(q):
        for way in (0, 1):
            side_copies[way, q].wait_recv()
            block = tok.at[rows_of(part(2 - way), 96, 96 * core), pl.ds(q * WINDOW, WINDOW)]
            core_copies[way, q] = launch(remote(
                block, block, tokc_s.at[way, q], tokc_r.at[way, q], other_core))

    def project(c, rows):
        start, width = CHUNKS[c]
        p_part[rows, pl.ds(start, width)] = lax.dot_general(
            tok[rows, :], gathered[start:start + width, :WIDTH], NT, preferred_element_type=F32)

    def offer(c):
        columns = pl.ds(*CHUNKS[c])
        for m in (1, 2):
            p_send[m - 1, :, columns] = p_part[rows_of(part(m)), columns].astype(BF16)
            p_copies[c, m] = launch(remote(
                p_send.at[m - 1, :, columns], p_recv.at[m - 1, :, columns],
                p_s.at[c, m - 1], p_r.at[c, m - 1], group_peer(m)))

    def activate(c):
        columns = pl.ds(*CHUNKS[c])
        for m in (1, 2):
            p_copies[c, m].wait_recv()
        projected = p_part[rows_of(j), columns] + p_recv[0, :, columns].astype(F32) + p_recv[1, :, columns].astype(F32)
        sig = 1.0 / (1.0 + jnp.exp(-projected))
        slope = sig * (1.0 + projected * (1.0 - sig))
        hidden[rows_of(j), columns] = (up_perm[:, columns] * slope).astype(BF16)
        block = hidden.at[rows_of(j), columns]
        for m in (1, 2):
            h_copies.append(launch(remote(
                block, block, h_s.at[c, m - 1], h_r.at[c, m - 1], group_peer(m))))
        act_perm[:, columns] = (projected * sig).astype(BF16)

    p_copies, h_copies = {}, []

    ring_arrive(0, 1)
    for u in (1, 2):
        a2a[2 - u].wait_recv()
        ring_open(u)
    def tell(n):
        step = 1 if n == 0 else 2
        greet(round_sem.at[n], [device(x, y, z + step, core), device(x, y, z + 12 - step, core)])

    def hear(n):
        pl.semaphore_wait(round_sem.at[n], 2)

    for n in (0, 2, 1):
        tokens_send(n)
    unpack(0)
    ring_arrive(0, 2)
    tokens_aside(0)
    ring_arrive(1, 1)
    tokens_aside(1)
    ring_arrive(2, 1)

    @pl.when(z == 0)
    def _():
        pl.semaphore_wait(end_sem, 2)

    tokens_send(3)
    tell(0)
    tokens_aside(2)
    unpack(1)
    unpack(-1)
    tokens_aside(3)
    tokens_across(0)
    ring_arrive(0, 3)
    tokens_across(1)
    tokens_across(2)
    ring_arrive(1, 2)
    tokens_across(3)
    ring_arrive(2, 2)
    unpack(2)
    unpack(-2)
    for copy in own_copies:
        copy.wait()
    project(0, rows_of(j))
    ring_arrive(0, 4)
    for copy in core_copies.values():
        copy.wait_recv()
    project(0, rows_of(part(1)))
    project(0, rows_of(part(2)))
    offer(0)
    ring_arrive(1, 3)
    ring_arrive(2, 3)
    hear(0)
    tell(1)
    unpack(3)
    unpack(-3)
    project(1, slice(None))
    offer(1)
    activate(0)
    ring_arrive(1, 4)
    ring_arrive(2, 4)
    hear(1)
    tell(2)
    unpack(4)
    project(2, slice(None))
    offer(2)
    activate(1)
    activate(2)
    act_out[...] = jnp.dot(act_perm[...], perm[...], preferred_element_type=F32).astype(BF16)
    for copy in h_copies:
        copy.wait_recv()

    quarters = [lax.rem(x + 2, 4), lax.rem(x + 1, 4), lax.rem(x + 3, 4), x]
    g_copies = []

    def half(i, rows, which):
        columns = pl.ds(pl.multiple_of(quarters[i] * WINDOW + 384 * which, 128), 384)
        return jnp.dot(hidden[rows, :], gathered[:, columns], preferred_element_type=F32)

    def give(i, rows):
        g_send[i, rows, :] = half(i, rows, 1 - core).astype(BF16)
        n = len(g_copies)
        g_copies.append(launch(remote(
            g_send.at[i, rows], g_recv.at[i, rows], g_s.at[n], g_r.at[n], other_core)))

    def keep(i):
        g_own[i] = half(i, pl.ds(0, 3 * ROWS), core)

    def pair_sum(i, rows):
        return g_own[i, rows, :] + g_recv[i, rows, :].astype(F32)

    pieces = 3 * ROWS // PIECE
    sides = (x + 1, x + 3)
    far_copies, near_copies, mid_copies = {}, {}, {}

    def rows_at(p, part_of=None):
        if part_of is None:
            return pl.ds(p * PIECE, PIECE)
        return pl.ds(p * PIECE + part_of * (PIECE // 2), PIECE // 2)

    def send_far(p):
        x_far[rows_at(p), :] = pair_sum(0, rows_at(p)).astype(BF16)
        for way in (0, 1):
            far_copies[p, way] = launch(remote(
                x_far.at[rows_at(p, way)], x_mid.at[rows_at(p, way)],
                m_s.at[p, way], m_r.at[p, way], device(sides[way], y, z, core)))

    def send_near(p):
        for way in (0, 1):
            rows = rows_at(p, 1 - way)
            x_send[way, rows, :] = pair_sum(1 + way, rows).astype(BF16)
            near_copies[p, way] = launch(remote(
                x_send.at[way, rows], x_recv.at[way, rows],
                n_s.at[p, way], n_r.at[p, way], device(sides[way], y, z, core)))

    def send_mid(p):
        for way in (0, 1):
            rows = rows_at(p, way)
            far_copies[p, way].wait_recv()
            x_send[way, rows, :] = (pair_sum(1 + way, rows) + x_mid[rows, :].astype(F32)).astype(BF16)
            mid_copies[p, way] = launch(remote(
                x_send.at[way, rows], x_recv.at[way, rows],
                x_s.at[p, way], x_r.at[p, way], device(sides[way], y, z, core)))

    leaving = []

    def send_owner(p):
        for way in (0, 1):
            near_copies[p, way].wait_recv()
            mid_copies[p, way].wait_recv()
        rows = rows_at(p)
        z_send[rows, :] = (
            pair_sum(3, rows) + x_recv[0, rows, :].astype(F32) + x_recv[1, rows, :].astype(F32)
        ).astype(BF16)
        s, there = p * PIECE // ROWS, p * PIECE % ROWS
        for i in range(3):
            block = 5 * j + 3 * core + i
            owner, side = block // 2, lax.rem(block, 2)
            valid = jnp.logical_or(core == 0, j == 2) if i == 2 else True
            here = jnp.logical_and(owner == z_hi * 2 + core, j == s)
            src = z_send.at[rows, pl.ds(128 * i, 128)]
            dst = z_recv.at[z_hi, pl.ds(there, PIECE), pl.ds(pl.multiple_of(128 * side, 128), 128)]
            arrived = f_r.at[z_hi, side, there // PIECE]
            away = remote(
                src, dst, f_s.at[p, i], arrived, {"inter": x * 8 + owner, "intra": s * 8 + y})
            stay = pltpu.make_async_copy(src, dst, arrived)
            leaves = jnp.logical_and(valid, jnp.logical_not(here))

            @pl.when(leaves)
            def _():
                away.start()

            @pl.when(jnp.logical_and(valid, here))
            def _():
                stay.start()

            leaving.append((leaves, away))

    every = pl.ds(0, 3 * ROWS)
    give(0, pl.ds(0, ROWS))
    give(0, pl.ds(ROWS, 2 * ROWS))
    keep(0)
    give(1, every)
    g_copies[0].wait_recv()
    send_far(0)
    send_far(1)
    give(2, every)
    g_copies[1].wait_recv()
    send_far(2)
    keep(1)
    keep(2)
    g_copies[2].wait_recv()
    g_copies[3].wait_recv()
    send_near(0)
    send_mid(0)
    send_near(1)
    send_mid(1)
    give(3, every)
    send_far(3)
    send_near(2)
    keep(3)
    g_copies[4].wait_recv()
    hear(2)
    send_owner(0)
    send_near(3)
    send_mid(2)
    send_owner(1)
    send_mid(3)
    send_far(4)
    send_far(5)
    send_near(4)
    send_owner(2)
    send_near(5)
    send_mid(4)
    send_owner(3)
    send_mid(5)
    send_owner(4)
    send_owner(5)

    for copy in pending + leaving_to[0] + leaving_to[1]:
        copy.wait_send()
    for condition, copies in token_sends:
        @pl.when(condition)
        def _():
            for copy in copies:
                copy.wait_send()
    for leaves, copy in leaving:
        @pl.when(leaves)
        def _():
            copy.wait_send()

    total = None
    for source in range(4):
        for side in range(2):
            for part_of in range(ROWS // PIECE):
                piece = z_recv.at[source, pl.ds(PIECE * part_of, PIECE), pl.ds(128 * side, 128)]
                pltpu.make_async_copy(piece, piece, f_r.at[source, side, part_of]).wait()
        value = z_recv[source].astype(F32)
        total = value if total is None else total + value
    grad_out[...] = total


def per_device(tokens, weight_codes, exponents, upstream):
    vmem = pl.BlockSpec(memory_space=pltpu.VMEM)
    hbm = pl.BlockSpec(memory_space=pltpu.HBM)
    dma = pltpu.SemaphoreType.DMA
    pieces = 3 * ROWS // PIECE
    return pl.pallas_call(
        kernel,
        out_shape=(
            jax.ShapeDtypeStruct((ROWS, 456), BF16),
            jax.ShapeDtypeStruct((ROWS, 256), F32),
        ),
        in_specs=[hbm] * 4,
        out_specs=(vmem, vmem),
        scratch_shapes=[
            pltpu.VMEM((19, 8192), BF16),
            pltpu.VMEM((19, 64), jnp.int32),
            pltpu.VMEM((ROWS, 456), BF16),
            pltpu.VMEM((3, 16, UNIT), BF16),
            pltpu.VMEM((3, 16, PACK), F32),
            pltpu.VMEM((512, UNIT), BF16),
            pltpu.VMEM((3 * ROWS, WIDTH), BF16),
            pltpu.VMEM((512, 456), BF16),
            pltpu.VMEM((ROWS, 512), F32),
            pltpu.VMEM((3 * ROWS, 512), F32),
            pltpu.VMEM((2, ROWS, 512), BF16),
            pltpu.VMEM((2, ROWS, 512), BF16),
            pltpu.VMEM((ROWS, 512), BF16),
            pltpu.VMEM((3 * ROWS, 512), BF16),
            pltpu.VMEM((4, 3 * ROWS, 384), BF16),
            pltpu.VMEM((4, 3 * ROWS, 384), BF16),
            pltpu.VMEM((4, 3 * ROWS, 384), F32),
            pltpu.VMEM((3 * ROWS, 384), BF16),
            pltpu.VMEM((2, 3 * ROWS, 384), BF16),
            pltpu.VMEM((3 * ROWS, 384), BF16),
            pltpu.VMEM((2, 3 * ROWS, 384), BF16),
            pltpu.VMEM((3 * ROWS, 384), BF16),
            pltpu.VMEM((4, ROWS, 256), BF16),
            pltpu.SemaphoreType.REGULAR, pltpu.SemaphoreType.REGULAR((3,)),
            dma((3,)), dma((4,)),
            dma((2,)), dma((2,)),
            dma((3, 2, 4)), dma((3, 2, 4)),
            dma((3, 4)), dma((2, 4)),
            dma((2, 4)), dma((2, 4)),
            dma((2, 4)), dma((2, 4)),
            dma((3, 2)), dma((3, 2)),
            dma((3, 2)), dma((3, 2)),
            dma((5,)), dma((5,)),
            dma((pieces, 2)), dma((pieces, 2)),
            dma((pieces, 2)), dma((pieces, 2)),
            dma((pieces, 2)), dma((pieces, 2)),
            dma((pieces, 3)), dma((4, 2, ROWS // PIECE)),
        ],
        compiler_params=pltpu.CompilerParams(
            collective_id=0, has_side_effects=True, vmem_limit_bytes=107 << 19),
        cost_estimate=pl.CostEstimate(
            flops=4 * ROWS * 8192 * 456, bytes_accessed=8 << 20, transcendentals=ROWS * 512),
    )(tokens, weight_codes, exponents, upstream)


def solution(mesh):
    placed = (
        P("intra", None),
        P(("inter", "intra"), None),
        P(("inter", "intra"), None),
        P("intra", "inter"),
    )
    return jax.shard_map(
        per_device,
        mesh=mesh,
        in_specs=placed,
        out_specs=(P("intra", "inter"), P("intra", "inter")),
        check_vma=False,
    )
```
